256 devices in a mesh: sec: 64 (over z, y, core), xs: 4 (over x).
Axes of the slice: x: 4, y: 4, z: 8, core: 2. Of those that a mesh axis runs over, the one named last changes fastest.
Arguments:
- q_block: float32 [512, 4, 8192], P('sec', None, 'xs'), may hold values from -0.0029296875 to 0.0029296875
- q_prev: float32 [512, 4, 8192], P('sec', None, 'xs'), may hold values from -0.0029296875 to 0.0029296875
- b_prev: float32 [4, 4], replicated, as said below
- stiff_blocks: float32 [64, 5, 128, 128], P('xs'), as said below
- couple_blocks: float32 [64, 5, 128, 128], P('xs'), as said below
- block_cols: int32 [64, 5], P('xs'), may hold values from 0 to 63, as said below
- assign: int32 [64], replicated, may hold values from 0 to 255, as said below
Outputs:
- q_next: float32 [512, 4, 8192], P('sec', None, 'xs')
- alphas: float32 [3, 4, 4], replicated
- betas: float32 [3, 4, 4], replicated
The draws below stay inside these ranges and needn't reach their ends.
Inputs may be any that keep to these rules, and one draw needn't show every extreme that they name: `block_cols`: slot k of block row r refers to offset k - 2: it holds r + k - 2 where that block is coupled and r itself otherwise; offsets -1, 0 and 1 are coupled wherever the column lies in the cross-section; coupling is symmetric between rows. `stiff_blocks`: block (r, k) is the transpose of block (r + k - 2, 4 - k); blocks of uncoupled slots are zero. `couple_blocks`: block (r, k) is the transpose of block (r + k - 2, 4 - k); blocks of uncoupled slots are zero. `b_prev`: upper triangular with a positive diagonal. `assign`: 64 different harmonics, among them 0 and 255.
All inputs are finite; a program needn't handle non-finite values.
Results may differ from the reference program's by a relative error of at most 0.0003.
Values sent between devices are 32-bit elements; how exact they have to be, the bound alone decides.
No kernel may reach another device: no remote copies, remote signals or barrier semaphores. Data moves between devices by JAX's collectives and lax.ppermute only.
A program may use at most 128 MiB of HBM per device.

```python
import math
import jax
import jax.numpy as jnp
from jax import lax

BLOCK = 128
COLS = 4
REACH = 2
ITERS = 3
NNZ = 5
SECTORS = 512
HARM = 64
NBLK = 64
DOF = 8192


def coupled_slots(key):
    bits = jax.random.randint(key, (REACH + 1, NBLK), 0, 2)
    offsets = jnp.arange(NNZ, dtype=jnp.int32) - REACH
    rows_all = jnp.arange(NBLK, dtype=jnp.int32)
    target = rows_all[:, None] + offsets[None, :]
    inside = (target >= 0) & (target < NBLK)
    edge = jnp.clip(jnp.minimum(rows_all[:, None], target), 0, NBLK - 1)
    chosen = bits[jnp.abs(offsets)[None, :], edge] == 1
    present = inside & ((jnp.abs(offsets)[None, :] <= 1) | chosen)
    return (present, target)


def symmetric_blocks(key, present, noise, diagonal):
    offsets = jnp.arange(NNZ, dtype=jnp.int32) - REACH
    rows_all = jnp.arange(NBLK, dtype=jnp.int32)
    raw = noise * jax.random.uniform(key, (NBLK, NNZ, BLOCK, BLOCK), jnp.float32, -1.0, 1.0)
    reverse = raw[:, ::-1]
    shifted = jnp.stack([reverse[jnp.clip(rows_all + offsets[k], 0, NBLK - 1), k] for k in range(NNZ)], 1)
    mirrored = jnp.swapaxes(shifted, 2, 3)
    side = offsets[None, :, None, None]
    blocks = jnp.where(side > 0, raw, jnp.where(side < 0, mirrored, 0.5 * (raw + mirrored)))
    blocks = blocks + jnp.where(side == 0, diagonal, 0.0) * jnp.eye(BLOCK, dtype=jnp.float32)
    return jnp.where(present[:, :, None, None], blocks, 0.0).astype(jnp.float32)


def draw_block_cols(key, part):
    present, target = coupled_slots(key)
    rows_all = jnp.arange(NBLK, dtype=jnp.int32)
    return jnp.where(present, target, rows_all[:, None]).astype(jnp.int32)


def draw_stiff_blocks(key, part):
    present, target = coupled_slots(key)
    key = jax.random.fold_in(key, 5)
    return symmetric_blocks(key, present, 0.9 / (NNZ * BLOCK) ** 0.5, 1.0)


def draw_couple_blocks(key, part):
    present, target = coupled_slots(key)
    key = jax.random.fold_in(key, 7)
    return symmetric_blocks(key, present, 1.4 / (NNZ * BLOCK) ** 0.5, -0.5)


def draw_b_prev(key, part):
    key = jax.random.fold_in(key, 11)
    first, second = jax.random.split(key)
    diagonal = jax.random.uniform(first, (COLS,), jnp.float32, 0.5, 1.5)
    upper = 0.3 * jax.random.normal(second, (COLS, COLS), jnp.float32)
    return (jnp.triu(upper, 1) + jnp.diag(diagonal)).astype(jnp.float32)


def draw_assign(key, part):
    key = jax.random.fold_in(key, 13)
    first, second = jax.random.split(key)
    middle = jax.random.permutation(first, jnp.arange(1, SECTORS // 2 - 1, dtype=jnp.int32))
    ends = jnp.array([0, SECTORS // 2 - 1], dtype=jnp.int32)
    picked = jnp.concatenate([ends, middle[:HARM - 2].astype(jnp.int32)])
    order = jax.random.permutation(second, jnp.arange(HARM, dtype=jnp.int32))
    return picked[order].astype(jnp.int32)


def steps_of(stream_key, shape, cuts, low, top_value):
    def one(dim, parts):
        draws = jax.random.uniform(jax.random.fold_in(jax.random.fold_in(stream_key, 6), dim), (parts,), jnp.float32, low / len(cuts), top_value / len(cuts))
        return jnp.repeat(jnp.exp(draws), shape[dim] // parts).reshape((-1,) + (1,) * (len(shape) - dim - 1))

    level = one(*cuts[0])
    for cut in cuts[1:]:
        level = level * one(*cut)
    return level


def normal_values(own_key, extent, scale, limit, cuts=(), kind=jnp.bfloat16):
    values = scale * jax.random.normal(own_key, extent, jnp.float32)
    if cuts:
        values = values * steps_of(own_key, extent, cuts, -0.22, 0.18)
    return jnp.clip(values, -limit, limit).astype(kind)


def setup_inputs(seed: int = 0) -> dict:
    keys = jax.random.split(jax.random.key(seed), 8)
    return {
        "q_block": normal_values(keys[0], (SECTORS, COLS, DOF), (SECTORS * DOF) ** -0.5, 0.0029296875, ((0, 64), (2, 4)), jnp.float32),
        "q_prev": normal_values(keys[1], (SECTORS, COLS, DOF), (SECTORS * DOF) ** -0.5, 0.0029296875, ((0, 64), (2, 4)), jnp.float32),
        "b_prev": draw_b_prev(jax.random.fold_in(keys[7], 71), 0),
        "stiff_blocks": draw_stiff_blocks(jax.random.fold_in(keys[7], 71), 0),
        "couple_blocks": draw_couple_blocks(jax.random.fold_in(keys[7], 71), 0),
        "block_cols": draw_block_cols(jax.random.fold_in(keys[7], 71), 0),
        "assign": draw_assign(jax.random.fold_in(keys[7], 71), 0),
    }


def spectrum_rows(assign, sectors, total):
    harmonic = jnp.repeat(assign, 2)
    parity = jnp.arange(harmonic.shape[0], dtype=jnp.int32) % 2
    phases = harmonic[:, None] * sectors[None, :] % total
    angles = 2.0 * math.pi / total * phases.astype(jnp.float32)
    weights = jnp.where(harmonic == 0, math.sqrt(1.0 / total), math.sqrt(2.0 / total)).astype(jnp.float32)
    values = jnp.where(parity[:, None] == 0, jnp.cos(angles), -jnp.sin(angles))
    return values * weights[:, None]

def harmonic_apply(field, stiff_blocks, couple_blocks, block_cols, factor):
    picked = field[:, block_cols]
    own = jnp.einsum('cnkj,nkij->cni', picked, stiff_blocks, precision=lax.Precision.HIGHEST)
    cross = jnp.einsum('cnkj,nkij->cni', picked, couple_blocks, precision=lax.Precision.HIGHEST)
    return own + factor * cross

def reference(q_block, q_prev, b_prev, stiff_blocks, couple_blocks, block_cols, assign):
    highest = lax.Precision.HIGHEST
    sectors = jnp.arange(SECTORS, dtype=jnp.int32)
    forward = spectrum_rows(assign, sectors, SECTORS)
    factors = jnp.cos(2.0 * math.pi / SECTORS * (assign % SECTORS).astype(jnp.float32))
    current, previous, coupling = (q_block, q_prev, b_prev)
    alpha_list = []
    beta_list = []
    for step in range(ITERS):
        flat = current.reshape(SECTORS, COLS * DOF)
        spectrum = jnp.dot(forward.astype(jnp.float32), flat.astype(jnp.float32), precision=highest, preferred_element_type=jnp.float32)
        fields = spectrum.reshape(HARM, 2 * COLS, NBLK, BLOCK)

        def one_slot(pair):
            return harmonic_apply(pair[0], stiff_blocks, couple_blocks, block_cols, pair[1])
        applied = lax.map(one_slot, (fields, factors)).reshape(2 * HARM, COLS * DOF)
        image = jnp.dot(forward.T.astype(jnp.float32), applied.astype(jnp.float32), precision=highest, preferred_element_type=jnp.float32)
        image = image.reshape(SECTORS, COLS, DOF)
        image = image - jnp.einsum('slp,il->sip', previous, coupling, precision=highest)
        block_alpha = jnp.einsum('sip,sjp->ij', current, image, precision=highest)
        residual = image - jnp.einsum('slp,li->sip', current, block_alpha, precision=highest)
        gram = jnp.einsum('sip,sjp->ij', residual, residual, precision=highest)
        lower = jnp.linalg.cholesky(gram)
        inverse = jax.scipy.linalg.solve_triangular(lower, jnp.eye(COLS, dtype=jnp.float32), lower=True)
        following = jnp.einsum('slp,il->sip', residual, inverse, precision=highest)
        alpha_list.append(block_alpha)
        beta_list.append(lower.T)
        previous, current, coupling = (current, following, lower.T)
    return (current, jnp.stack(alpha_list), jnp.stack(beta_list))
```

```python
import math

import jax
import jax.numpy as jnp
from jax import lax
from jax.experimental import pallas as pl
from jax.experimental.pallas import tpu as pltpu
from jax.sharding import Mesh
from jax.sharding import PartitionSpec as P

HI = lax.Precision.HIGHEST
SEC = ("z", "y", "core")
BLOCKS = ("z", "core", "xs")
SECTORS = 512
NT = (((1,), (1,)), ((), ()))
VMEM_LIMIT = 32 * 1024 * 1024


def call(kernel, out, *args, specs=None, **kw):
    return pl.pallas_call(
        kernel,
        out_shape=out,
        compiler_params=pltpu.CompilerParams(vmem_limit_bytes=VMEM_LIMIT),
        **kw,
    )(*args)


def f32(*shape):
    return jax.ShapeDtypeStruct(shape, jnp.float32)


def dot(a, b, dims=(((1,), (0,)), ((), ()))):
    return lax.dot_general(a, b, dims, precision=HI, preferred_element_type=jnp.float32)


def pack_kernel(q_ref, p_ref, out_ref, gram_ref):
    for block in range(16):
        for col in range(4):
            place = (block // 2 * 4 + col) * 2 + block % 2
            lanes = pl.ds(block * 128, 128)
            out_ref[place, 0] = q_ref[:, col, lanes]
            out_ref[place, 1] = p_ref[:, col, lanes]
    total = jnp.zeros((8, 8), jnp.float32)
    for s in range(8):
        rows = jnp.concatenate([q_ref[s], p_ref[s]], axis=0)
        total += dot(rows, rows, NT)
    gram_ref[...] = jnp.zeros((8, 128), jnp.float32)
    gram_ref[:, 64:72] = total


def stats_kernel(s_ref, c_ref, out_ref):
    step = pl.program_id(0)
    row = lax.broadcasted_iota(jnp.int32, (128, 128), 0)
    col = lax.broadcasted_iota(jnp.int32, (128, 128), 1)
    big = jnp.float32(3.0e38)
    found = []
    for ref in (s_ref, c_ref):
        largest = jnp.max(jnp.abs(ref[0]), axis=0)
        largest = jnp.max(largest.reshape(16, 8, 128), axis=0)
        middle = ref[0, 2]
        top = jnp.max(jnp.where(row == col, middle, -big).reshape(16, 8, 128), axis=0)
        low = jnp.max(jnp.where(row == col, -middle, -big).reshape(16, 8, 128), axis=0)
        found += [largest, top, low]

    @pl.when(step == 0)
    def _():
        for i, v in enumerate(found):
            out_ref[i] = v

    @pl.when(step > 0)
    def _():
        for i, v in enumerate(found):
            out_ref[i] = jnp.maximum(out_ref[i], v)


def forward_kernel(f_ref, r_ref, out_ref):
    for t in range(2):
        field = r_ref[:, t].reshape(SECTORS, 128)
        out_ref[:, t] = dot(f_ref[...], field).reshape(4, 32, 128)


def inverse_kernel(f_ref, r_ref, out_ref):
    field = r_ref[...].reshape(128, 128)
    out_ref[...] = dot(f_ref[...], field, (((0,), (0,)), ((), ()))).reshape(64, 8, 128)


def apply_kernel(order, index_ref, m2, m1, v0, p1, p2, s_ref, c_ref, f_ref, k_ref, out_ref):
    def rows(ref):
        if order == "ct":
            return jnp.concatenate([ref[:, 0].reshape(128, 128), ref[:, 1].reshape(128, 128)], 0)
        return ref[...].reshape(-1, 128)

    own = rows(v0)
    count = own.shape[0]
    left = jnp.concatenate([rows(m2), rows(m1), own, rows(p1), rows(p2)], axis=1)
    right = jnp.concatenate(
        [
            jnp.concatenate([s_ref[0, k] for k in range(5)], axis=1),
            jnp.concatenate([c_ref[0, k] for k in range(5)], axis=1),
        ],
        axis=0,
    )
    both = dot(left, right, NT)
    factor = f_ref[...][None]
    value = both[:, :128].reshape(-1, 32, 128) + factor * both[:, 128:].reshape(-1, 32, 128)
    value = (value - k_ref[0:1, :][None] * own.reshape(-1, 32, 128)) * k_ref[1:2, :][None]
    out_ref[...] = value.reshape(out_ref.shape)


def apply_op(order, parts, stiff, couple, factor, scales, block, out_shape):
    whole = pl.BlockSpec(memory_space=pltpu.VMEM)
    picked = pl.BlockSpec((1, 5, 128, 128), lambda i, b: (b[0], 0, 0, 0))
    return pl.pallas_call(
        lambda *refs: apply_kernel(order, *refs),
        out_shape=f32(*out_shape),
        grid_spec=pltpu.PrefetchScalarGridSpec(
            num_scalar_prefetch=1,
            grid=(1,),
            in_specs=[whole] * 5 + [picked, picked, whole, whole],
            out_specs=whole,
        ),
        compiler_params=pltpu.CompilerParams(vmem_limit_bytes=VMEM_LIMIT),
    )(block, *parts, stiff, couple, factor, scales)


def gram_kernel(k0, k1, k2, k3, m_ref, out_ref):
    total = jnp.zeros((32, 32), jnp.float32)
    for r in range(32):
        rows = jnp.concatenate(
            [
                k0[:, 0, r, :],
                k0[:, 1, r, :],
                k1[0, :, r, :],
                k1[1, :, r, :],
                k2[0, :, r, :],
                k2[1, :, r, :],
                k3[:, r, :],
                jnp.zeros((4, 128), jnp.float32),
            ],
            axis=0,
        )
        total += dot(rows, rows, NT)
    out_ref[...] = jnp.zeros((32, 128), jnp.float32)
    out_ref[:, 0:32] = total
    out_ref[0:8, 64:128] = m_ref[:, 64:128]


def mixed(weights, rows):
    total = weights[:, 0:1] * rows[0:1, :]
    for l in range(1, 4):
        total += weights[:, l : l + 1] * rows[l : l + 1, :]
    return total


def solve_kernel(g_ref, b_ref, k_ref, k0, k1, k2, k3, z_ref, coef_ref, alpha_ref, beta_ref):
    lane = lax.broadcasted_iota(jnp.int32, (4, 128), 1)
    row = lax.broadcasted_iota(jnp.int32, (4, 128), 0)
    spectral = lane < 28
    sigma, scale = k_ref[0:1, :], k_ref[2:3, :]
    full = g_ref[...]
    wide = lax.broadcasted_iota(jnp.int32, (32, 128), 1)
    gram = jnp.where(wide < 28, full, 0.0)
    shifted = jnp.concatenate([gram[8:32], jnp.zeros((8, 128), jnp.float32)], axis=0)
    rest = jnp.where(
        (wide[0:8] >= 64) & (wide[0:8] < 72), full[0:8] - pltpu.roll(full[0:8], 64, 1), 0.0
    )
    first = gram[0:8] + rest
    cur = ((lane == row) | (lane == row + 64)).astype(jnp.float32)
    prev = ((lane == row + 4) | (lane == row + 68)).astype(jnp.float32)
    cur_g, prev_g = first[0:4], first[4:8]
    coupling = b_ref[...]
    for step in range(3):
        seen = jnp.where(spectral, cur, 0.0)
        w = scale * pltpu.roll(seen, 8, 1) + sigma * seen - mixed(coupling, prev)
        w_g = (
            scale * dot(cur[:, 0:32], shifted)
            + sigma * jnp.where(spectral, cur_g, 0.0)
            - mixed(coupling, prev_g)
        )
        turned = jnp.concatenate(
            [jnp.sum(w_g * cur[l : l + 1, :], axis=1, keepdims=True) for l in range(4)], axis=1
        )
        alpha_ref[step] = jnp.concatenate(
            [jnp.sum(cur_g * w[l : l + 1, :], axis=1, keepdims=True) for l in range(4)], axis=1
        )
        r = w - mixed(turned, cur)
        r_g = w_g - mixed(turned, cur_g)
        square = jnp.concatenate(
            [jnp.sum(r_g * r[l : l + 1, :], axis=1, keepdims=True) for l in range(4)], axis=1
        )
        small_row = lax.broadcasted_iota(jnp.int32, (4, 4), 0)
        small_col = lax.broadcasted_iota(jnp.int32, (4, 4), 1)
        pivots = jnp.zeros((4, 1), jnp.float32)
        one_row = lax.broadcasted_iota(jnp.int32, (4, 1), 0)
        for i in range(4):
            pivot = square[i : i + 1, i : i + 1]
            pivots = jnp.where(one_row == i, pivot, pivots)
            if i < 3:
                times = jnp.where(one_row > i, square[:, i : i + 1] / pivot, 0.0)
                r = r - times * r[i : i + 1, :]
                r_g = r_g - times * r_g[i : i + 1, :]
                square = square - times * square[i : i + 1, :]
        root = 1.0 / jnp.sqrt(pivots)
        upper = jnp.where(small_col >= small_row, square * root, 0.0)
        beta_ref[step] = upper
        prev, prev_g, coupling = cur, cur_g, upper
        cur, cur_g = r * root, r_g * root
    coef_ref[...] = cur
    weights = cur - jnp.where(lane < 8, pltpu.roll(cur, 64, 1), 0.0)
    basis = (
        [k0[c, 0] for c in range(4)]
        + [k0[c, 1] for c in range(4)]
        + [k1[t, c] for t in range(2) for c in range(4)]
        + [k2[t, c] for t in range(2) for c in range(4)]
        + [k3[c] for c in range(4)]
    )
    for i in range(4):
        total = weights[i : i + 1, 0:1] * basis[0]
        for k in range(1, 28):
            total += weights[i : i + 1, k : k + 1] * basis[k]
        z_ref[i] = total


def last_kernel(r_ref, q_ref, coef_ref, out_ref):
    coef = coef_ref[...]
    scalars = [
        [coef[c : c + 1, 64 + k : 65 + k] + jnp.zeros((8, 128), jnp.float32) for k in range(8)]
        for c in range(4)
    ]
    for block in range(16):
        places = [(block // 2 * 4 + c) * 2 + block % 2 for c in range(4)]
        tiles = [q_ref[p, 0] for p in places] + [q_ref[p, 1] for p in places]
        for c in range(4):
            total = r_ref[places[c]]
            for k in range(8):
                total += scalars[c][k] * tiles[k]
            out_ref[:, c, pl.ds(block * 128, 128)] = total


def table(assign):
    harmonic = jnp.repeat(assign, 2)
    parity = jnp.arange(harmonic.shape[0], dtype=jnp.int32) % 2
    sectors = jnp.arange(SECTORS, dtype=jnp.int32)
    phases = (harmonic[:, None] * sectors[None, :] + 128 * parity[:, None]) % SECTORS
    weights = jnp.where(harmonic == 0, math.sqrt(1.0 / SECTORS), math.sqrt(2.0 / SECTORS))
    weights = jnp.where((harmonic == 0) & (parity == 1), 0.0, weights).astype(jnp.float32)
    return jnp.cos(2.0 * math.pi / SECTORS * phases.astype(jnp.float32)) * weights[:, None]


def neighbour(value, offset):
    pairs = []
    for b in range(64):
        if 0 <= b + offset < 64:
            place = [(i % 16) * 4 + i // 16 for i in (b, b + offset)]
            pairs.append(tuple(place))
    return lax.ppermute(value, BLOCKS, pairs)


def around(value):
    return [neighbour(value, 2), neighbour(value, 1), value, neighbour(value, -1), neighbour(value, -2)]


def exchange(value, axis, count, step, combine):
    return combine(value, lax.ppermute(value, axis, [(i, i ^ step) for i in range(count)]))


def per_device(q_block, q_prev, b_prev, stiff_blocks, couple_blocks, block_cols, assign):
    block = lax.axis_index("z") * 2 + lax.axis_index("core")
    group = lax.axis_index("y")
    forward = table(assign)
    factors = jnp.cos(2.0 * math.pi / SECTORS * assign.astype(jnp.float32))
    mine = lax.dynamic_slice_in_dim(factors, group * 16, 16)
    factor = jnp.broadcast_to(jnp.repeat(mine, 2)[:, None], (32, 128))

    found = pl.pallas_call(
        stats_kernel,
        out_shape=f32(6, 8, 128),
        grid=(16,),
        in_specs=[pl.BlockSpec((1, 5, 128, 128), lambda i: (i, 0, 0, 0))] * 2,
        out_specs=pl.BlockSpec((6, 8, 128), lambda i: (0, 0, 0)),
        compiler_params=pltpu.CompilerParams(vmem_limit_bytes=VMEM_LIMIT),
    )(stiff_blocks, couple_blocks)
    found = jnp.broadcast_to(jnp.max(found, axis=(1, 2))[:, None], (6, 128))
    found = exchange(found, "xs", 4, 1, jnp.maximum)
    found = exchange(found, "xs", 4, 2, jnp.maximum)
    sigma = 0.5 * (found[1] - found[2]) + jnp.mean(factors) * (0.5 * (found[4] - found[5]))
    scale = found[0] + found[3]
    scale = jnp.where(scale > 0, scale, 1.0)
    scales = jnp.stack([sigma, 1.0 / scale, scale] + [scale] * 5)

    packed, gram_raw = call(pack_kernel, (f32(64, 2, 8, 128), f32(8, 128)), q_block, q_prev)
    received = lax.all_to_all(packed, SEC, 0, 0, tiled=True)
    spectrum = call(forward_kernel, f32(4, 2, 32, 128), forward, received)
    k0 = lax.all_to_all(spectrum, "y", 0, 0, tiled=True)
    where = block.astype(jnp.int32).reshape(1)
    k1 = apply_op("ct", around(k0), stiff_blocks, couple_blocks, factor, scales, where, (2, 4, 32, 128))
    k2 = apply_op("tc", around(k1), stiff_blocks, couple_blocks, factor, scales, where, (2, 4, 32, 128))
    k3 = apply_op("tc", around(k2[0]), stiff_blocks, couple_blocks, factor, scales, where, (4, 32, 128))
    gram = call(gram_kernel, f32(32, 128), k0, k1, k2, k3, gram_raw)
    for axis, count in (("core", 2), ("xs", 4), ("y", 4), ("z", 8)):
        step = 1
        while step < count:
            gram = exchange(gram, axis, count, step, jnp.add)
            step *= 2
    mix, coef, alphas, betas = call(
        solve_kernel,
        (f32(4, 32, 128), f32(4, 128), f32(3, 4, 4), f32(3, 4, 4)),
        gram, b_prev, scales, k0, k1, k2, k3,
    )
    rows = lax.all_to_all(mix, "y", 0, 0, tiled=True)
    image = call(inverse_kernel, f32(64, 8, 128), forward, rows)
    back = lax.all_to_all(image, SEC, 0, 0, tiled=True)
    out = call(last_kernel, f32(8, 4, 2048), back, packed, coef)
    return out, alphas, betas


def solution(mesh):
    fine = Mesh(mesh.devices.reshape(8, 4, 2, 4), ("z", "y", "core", "xs"))
    in_specs = (
        P(SEC, None, "xs"),
        P(SEC, None, "xs"),
        P(),
        P("xs", None, None, None),
        P("xs", None, None, None),
        P("xs", None),
        P(),
    )
    out_specs = (P(SEC, None, "xs"), P(), P())
    return jax.shard_map(
        per_device, mesh=fine, in_specs=in_specs, out_specs=out_specs, check_vma=False
    )
```

```python
import math

import jax
import jax.numpy as jnp
from jax import lax
from jax.experimental import pallas as pl
from jax.experimental.pallas import tpu as pltpu
from jax.sharding import Mesh
from jax.sharding import PartitionSpec as P

HI = lax.Precision.HIGHEST
SEC = ("z", "y", "core")
GROUP = ("y", "core")
RING = ("z", "xs")
SECTORS = 512
NT = (((1,), (1,)), ((), ()))
TN = (((0,), (0,)), ((), ()))
VMEM_LIMIT = 32 * 1024 * 1024


def f32(*shape):
    return jax.ShapeDtypeStruct(shape, jnp.float32)


def dot(a, b, dims=(((1,), (0,)), ((), ()))):
    return lax.dot_general(a, b, dims, precision=HI, preferred_element_type=jnp.float32)


def call(kernel, out, *args, scalar=None, **kw):
    whole = pl.BlockSpec(memory_space=pltpu.VMEM)
    specs = [whole] * len(args)
    if scalar is not None:
        specs = [pl.BlockSpec(memory_space=pltpu.SMEM)] + specs
        args = (scalar,) + args
    return pl.pallas_call(
        kernel,
        out_shape=out,
        in_specs=specs,
        out_specs=jax.tree.map(lambda _: whole, out),
        compiler_params=pltpu.CompilerParams(vmem_limit_bytes=VMEM_LIMIT),
        **kw,
    )(*args)


def turned(pair, flip):
    return pair + flip * (7 - 2 * pair)


def pack_kernel(flip_ref, q_ref, p_ref, out_ref):
    flip = flip_ref[0]
    for pair in range(8):
        place = turned(pair, flip) * 8
        lanes = pl.ds(pair * 256, 256)
        for col in range(4):
            out_ref[place + col] = q_ref[:, col, lanes]
            out_ref[place + 4 + col] = p_ref[:, col, lanes]


def raw_kernel(q_ref, p_ref, gram_ref):
    total = jnp.zeros((8, 8), jnp.float32)
    for s in range(8):
        rows = jnp.concatenate([q_ref[s], p_ref[s]], axis=0)
        total += dot(rows, rows, NT)
    gram_ref[...] = jnp.zeros((8, 128), jnp.float32)
    gram_ref[:, 0:8] = total


def stats_kernel(pair_ref, s_ref, c_ref, out_ref, own_ref):
    step = pl.program_id(0)
    row = lax.broadcasted_iota(jnp.int32, (128, 128), 0)
    col = lax.broadcasted_iota(jnp.int32, (128, 128), 1)
    big = jnp.float32(3.0e38)
    found = []
    for ref in (s_ref, c_ref):
        largest = jnp.max(jnp.abs(ref[0]), axis=0)
        largest = jnp.max(largest.reshape(16, 8, 128), axis=0)
        middle = ref[0, 2]
        top = jnp.max(jnp.where(row == col, middle, -big).reshape(16, 8, 128), axis=0)
        low = jnp.max(jnp.where(row == col, -middle, -big).reshape(16, 8, 128), axis=0)
        found += [largest, top, low]

    @pl.when(step == 0)
    def _():
        for i, v in enumerate(found):
            out_ref[i] = v

    @pl.when(step > 0)
    def _():
        for i, v in enumerate(found):
            out_ref[i] = jnp.maximum(out_ref[i], v)

    for half in range(2):

        @pl.when(step == pair_ref[0] * 2 + half)
        def _():
            for k in range(5):
                lanes = pl.ds(k * 128, 128)
                own_ref[half, 0:128, lanes] = s_ref[0, k]
                own_ref[half, 128:256, lanes] = c_ref[0, k]


def forward_kernel(f_ref, r_ref, out_ref):
    out_ref[...] = dot(f_ref[...], r_ref[...].reshape(SECTORS, 256)).reshape(8, 16, 256)


def apply_kernel(shift, left_ref, own_ref, right_ref, w_ref, f_ref, k_ref, *out_refs):
    count = own_ref.shape[0]
    rows = count * 16
    own = own_ref[...].reshape(rows, 256)
    wide = jnp.concatenate(
        [left_ref[...].reshape(rows, 256), own, right_ref[...].reshape(rows, 256)], axis=1
    )
    factor = f_ref[...][None]
    sigma, inverse = k_ref[0:1, :][None], k_ref[1:2, :][None]
    for half in range(2):
        both = dot(wide[:, half * 128 : half * 128 + 640], w_ref[half], NT)
        value = both[:, :128].reshape(count, 16, 128)
        value = value + factor * both[:, 128:].reshape(count, 16, 128)
        if shift:
            mine = own[:, half * 128 : half * 128 + 128].reshape(count, 16, 128)
            value = value - sigma * mine
        value = value * inverse
        size = count // len(out_refs)
        for i, ref in enumerate(out_refs):
            ref[:, :, half * 128 : half * 128 + 128] = value[i * size : (i + 1) * size]


def share_kernel(k0, k1, k2x, k2y, k3, raw_ref, out_ref):
    total = jnp.zeros((32, 32), jnp.float32)
    for r in range(16):
        rows = jnp.concatenate(
            [k0[:, r, :], k1[:, r, :], k2x[:, r, :], k2y[:, r, :], k3[:, r, :], jnp.zeros((4, 256), jnp.float32)],
            axis=0,
        )
        total += dot(rows, rows, NT)
    first = jnp.concatenate([raw_ref[:, 0:8], total[0:8, 8:32]], axis=1)
    packed = jnp.concatenate([first, total[8:16], total[16:24], total[24:32]], axis=1)
    group = lax.broadcasted_iota(jnp.int32, (16, 128), 1) // 32
    sets = (
        [k1[c] for c in range(4)],
        [k1[4 + c] for c in range(4)],
        [k2x[c] for c in range(4)],
        [k2y[c] for c in range(4)],
        [k3[c] for c in range(4)],
    )
    for m, columns in enumerate(sets):
        for half in range(2):
            tiles = [v[:, half * 128 : half * 128 + 128] for v in columns]
            for q in range(4):
                value = None
                for c in range(4):
                    by = (c - q) % 4 * 32
                    moved = pltpu.roll(tiles[c], by, 1) if by else tiles[c]
                    value = moved if value is None else jnp.where(group == c, moved, value)
                out_ref[half * 4 + q, m * 16 : m * 16 + 16] = value
    for d in range(8):
        out_ref[d, 80:88] = packed


def total_kernel(v_ref, out_ref):
    total = v_ref[0, 80:88]
    for d in range(1, 8):
        total += v_ref[d, 80:88]
    for d in range(32):
        out_ref[d] = total


def mixed(weights, rows):
    total = weights[:, 0:1] * rows[0:1, :]
    for l in range(1, 4):
        total += weights[:, l : l + 1] * rows[l : l + 1, :]
    return total


def products(a, b):
    return jnp.concatenate(
        [jnp.sum(a * b[l : l + 1, :], axis=1, keepdims=True) for l in range(4)], axis=1
    )


def solve_kernel(g_ref, b_ref, k_ref, v_ref, f_ref, image_ref, coef_ref, alpha_ref, beta_ref):
    lane = lax.broadcasted_iota(jnp.int32, (4, 128), 1)
    row = lax.broadcasted_iota(jnp.int32, (4, 128), 0)
    sigma, scale = k_ref[0:1, :], k_ref[2:3, :]
    packed = g_ref[0]
    for d in range(1, 32):
        packed += g_ref[d]
    narrow = lax.broadcasted_iota(jnp.int32, (8, 128), 1) < 32
    gram = jnp.concatenate(
        [
            jnp.where(narrow, packed if q == 0 else pltpu.roll(packed, 128 - 32 * q, 1), 0.0)
            for q in range(4)
        ],
        axis=0,
    )
    cur = (lane == row).astype(jnp.float32)
    prev = (lane == row + 4).astype(jnp.float32)
    cur_g, prev_g = gram[0:4], gram[4:8]
    coupling = b_ref[...]
    one_row = lax.broadcasted_iota(jnp.int32, (4, 1), 0)
    small_row = lax.broadcasted_iota(jnp.int32, (4, 4), 0)
    small_col = lax.broadcasted_iota(jnp.int32, (4, 4), 1)
    for step in range(3):
        moved = scale * pltpu.roll(jnp.where(lane < 20, cur, 0.0), 8, 1)
        moved += sigma * jnp.where(lane >= 8, cur, 0.0)
        w = moved - mixed(coupling, prev)
        w_g = dot(moved[:, 0:32], gram) - mixed(coupling, prev_g)
        across = products(w_g, cur)
        alpha_ref[step] = products(cur_g, w)
        r = w - mixed(across, cur)
        r_g = w_g - mixed(across, cur_g)
        square = products(r_g, r)
        pivots = jnp.zeros((4, 1), jnp.float32)
        for i in range(4):
            pivot = square[i : i + 1, i : i + 1]
            pivots = jnp.where(one_row == i, pivot, pivots)
            if i < 3:
                times = jnp.where(one_row > i, square[:, i : i + 1] / pivot, 0.0)
                r = r - times * r[i : i + 1, :]
                r_g = r_g - times * r_g[i : i + 1, :]
                square = square - times * square[i : i + 1, :]
        root = 1.0 / jnp.sqrt(pivots)
        upper = jnp.where(small_col >= small_row, square * root, 0.0)
        beta_ref[step] = upper
        prev, prev_g, coupling = cur, cur_g, upper
        cur, cur_g = r * root, r_g * root
    coef_ref[...] = cur
    spread = (lane // 32 == row).astype(jnp.float32)
    weights = dot(cur, spread, TN)
    same = lax.broadcasted_iota(jnp.int32, (32, 128), 1) % 32 == lax.broadcasted_iota(jnp.int32, (32, 128), 0)
    mixing = jnp.concatenate([jnp.where(same, weights[8 + k : 9 + k, :], 0.0) for k in range(20)], axis=0)
    vectors = jnp.concatenate([v_ref[:, m * 16 : m * 16 + 16].reshape(128, 128) for m in range(5)], axis=1)
    field = dot(vectors, mixing)
    image_ref[...] = dot(f_ref[...], field, TN).reshape(64, 8, 128)


def base_kernel(flip_ref, q_ref, coef_ref, out_ref):
    flip = flip_ref[0]
    coef = coef_ref[...]
    scalars = [
        [coef[c : c + 1, k : k + 1] + jnp.zeros((8, 256), jnp.float32) for k in range(8)]
        for c in range(4)
    ]
    for pair in range(8):
        place = turned(pair, flip) * 8
        tiles = [q_ref[place + k] for k in range(8)]
        for c in range(4):
            total = scalars[c][0] * tiles[0]
            for k in range(1, 8):
                total += scalars[c][k] * tiles[k]
            out_ref[pair, c] = total


def last_kernel(flip_ref, r_ref, base_ref, out_ref):
    flip = flip_ref[0]
    group = lax.broadcasted_iota(jnp.int32, (8, 128), 1) // 32
    for pair in range(8):
        place = turned(pair, flip) * 8
        for half in range(2):
            tiles = [r_ref[place + half * 4 + q] for q in range(4)]
            for c in range(4):
                value = None
                for q in range(4):
                    by = (q - c) % 4 * 32
                    moved = pltpu.roll(tiles[q], by, 1) if by else tiles[q]
                    value = moved if value is None else jnp.where(group == q, moved, value)
                value += base_ref[pair, c, :, half * 128 : half * 128 + 128]
                out_ref[:, c, pl.ds(pair * 256 + half * 128, 128)] = value


def table(assign):
    harmonic = jnp.repeat(assign, 2)
    parity = jnp.arange(harmonic.shape[0], dtype=jnp.int32) % 2
    sectors = jnp.arange(SECTORS, dtype=jnp.int32)
    phases = (harmonic[:, None] * sectors[None, :] + 128 * parity[:, None]) % SECTORS
    weights = jnp.where(harmonic == 0, math.sqrt(1.0 / SECTORS), math.sqrt(2.0 / SECTORS))
    weights = jnp.where((harmonic == 0) & (parity == 1), 0.0, weights).astype(jnp.float32)
    return jnp.cos(2.0 * math.pi / SECTORS * phases.astype(jnp.float32)) * weights[:, None]


def ring_place(pair):
    slab, at = pair // 8 % 4, pair % 8
    return (at if slab % 2 == 0 else 7 - at) * 4 + slab


def beside(value):
    after = [(ring_place(i), ring_place(i + 1)) for i in range(32)]
    before = [(j, i) for i, j in after]
    return lax.ppermute(value, RING, after), lax.ppermute(value, RING, before)


def highest(value, step):
    return jnp.maximum(value, lax.ppermute(value, "xs", [(i, i ^ step) for i in range(4)]))


def per_device(q_block, q_prev, b_prev, stiff_blocks, couple_blocks, block_cols, assign):
    flip = (lax.axis_index("xs") % 2).astype(jnp.int32).reshape(1)
    pair = turned(lax.axis_index("z"), flip)
    group = lax.axis_index("y") * 2 + lax.axis_index("core")

    packed = call(pack_kernel, f32(64, 8, 256), q_block, q_prev, scalar=flip)
    received = lax.all_to_all(packed, SEC, 0, 0, tiled=True)

    forward = table(assign)
    factors = jnp.cos(2.0 * math.pi / SECTORS * assign.astype(jnp.float32))
    mine = lax.dynamic_slice_in_dim(factors, group * 8, 8)
    factor = jnp.broadcast_to(jnp.repeat(mine, 2)[:, None], (16, 128))
    raw = call(raw_kernel, f32(8, 128), q_block, q_prev)
    found, own = pl.pallas_call(
        stats_kernel,
        out_shape=(f32(6, 8, 128), f32(2, 256, 640)),
        grid_spec=pltpu.PrefetchScalarGridSpec(
            num_scalar_prefetch=1,
            grid=(16,),
            in_specs=[pl.BlockSpec((1, 5, 128, 128), lambda i, p: (i, 0, 0, 0))] * 2,
            out_specs=(
                pl.BlockSpec((6, 8, 128), lambda i, p: (0, 0, 0)),
                pl.BlockSpec((2, 256, 640), lambda i, p: (0, 0, 0)),
            ),
        ),
        compiler_params=pltpu.CompilerParams(vmem_limit_bytes=VMEM_LIMIT),
    )(pair, stiff_blocks, couple_blocks)
    found = jnp.broadcast_to(jnp.max(found, axis=(1, 2))[:, None], (6, 128))
    found = highest(highest(found, 1), 2)
    sigma = 0.5 * (found[1] - found[2]) + jnp.mean(factors) * (0.5 * (found[4] - found[5]))
    scale = found[0] + found[3]
    scale = jnp.where(scale > 0, scale, 1.0)
    scales = jnp.stack([sigma, 1.0 / scale, scale] + [scale] * 5)

    spectrum = call(forward_kernel, f32(8, 16, 256), forward, received)
    k0 = lax.all_to_all(spectrum, GROUP, 0, 0, tiled=True)

    def operator(value, shift, out):
        left, right = beside(value)
        return call(
            lambda *refs: apply_kernel(shift, *refs), out, left, value, right, own, factor, scales
        )

    (k1,) = operator(k0, False, (f32(8, 16, 256),))
    k2x, k2y = operator(k1, True, (f32(4, 16, 256), f32(4, 16, 256)))
    (k3,) = operator(k2x, True, (f32(4, 16, 256),))

    shares = call(share_kernel, f32(8, 88, 128), k0, k1, k2x, k2y, k3, raw)
    vectors = lax.all_to_all(shares, GROUP, 0, 0, tiled=True)
    grams = lax.all_to_all(call(total_kernel, f32(32, 8, 128), vectors), RING, 0, 0, tiled=True)
    image, coef, alphas, betas = call(
        solve_kernel,
        (f32(64, 8, 128), f32(4, 128), f32(3, 4, 4), f32(3, 4, 4)),
        grams, b_prev, scales, vectors, forward,
    )
    back = lax.all_to_all(image, SEC, 0, 0, tiled=True)
    base = call(base_kernel, f32(8, 4, 8, 256), packed, coef, scalar=flip)
    out = call(last_kernel, f32(8, 4, 2048), back, base, scalar=flip)
    return out, alphas, betas


def solution(mesh):
    fine = Mesh(mesh.devices.reshape(8, 4, 2, 4), ("z", "y", "core", "xs"))
    in_specs = (
        P(SEC, None, "xs"),
        P(SEC, None, "xs"),
        P(),
        P("xs", None, None, None),
        P("xs", None, None, None),
        P("xs", None),
        P(),
    )
    out_specs = (P(SEC, None, "xs"), P(), P())
    return jax.shard_map(
        per_device, mesh=fine, in_specs=in_specs, out_specs=out_specs, check_vma=False
    )
```

```python
import math

import jax
import jax.numpy as jnp
from jax import lax
from jax.experimental import pallas as pl
from jax.experimental.pallas import tpu as pltpu
from jax.sharding import Mesh
from jax.sharding import PartitionSpec as P

HI = lax.Precision.HIGHEST
SEC = ("z", "y", "core")
GROUP = ("y", "core")
RING = ("z", "xs")
SECTORS = 512
NT = (((1,), (1,)), ((), ()))
TN = (((0,), (0,)), ((), ()))
VMEM_LIMIT = 32 * 1024 * 1024


def f32(*shape):
    return jax.ShapeDtypeStruct(shape, jnp.float32)


def dot(a, b, dims=(((1,), (0,)), ((), ()))):
    return lax.dot_general(a, b, dims, precision=HI, preferred_element_type=jnp.float32)


def bf16(*shape):
    return jax.ShapeDtypeStruct(shape, jnp.bfloat16)


def split(value):
    high = value.astype(jnp.bfloat16)
    return high, (value - high.astype(jnp.float32)).astype(jnp.bfloat16)


def fast(a, b):
    return lax.dot_general(a, b, (((1,), (0,)), ((), ())), preferred_element_type=jnp.float32)


def call(kernel, out, *args, scalar=None, **kw):
    whole = pl.BlockSpec(memory_space=pltpu.VMEM)
    specs = [whole] * len(args)
    if scalar is not None:
        specs = [pl.BlockSpec(memory_space=pltpu.SMEM)] + specs
        args = (scalar,) + args
    return pl.pallas_call(
        kernel,
        out_shape=out,
        in_specs=specs,
        out_specs=jax.tree.map(lambda _: whole, out),
        compiler_params=pltpu.CompilerParams(vmem_limit_bytes=VMEM_LIMIT),
        **kw,
    )(*args)


def turned(pair, flip):
    return pair + flip * (7 - 2 * pair)


def pack_kernel(flip_ref, q_hbm, p_hbm, out_hbm, q_ref, p_ref, o_ref, in_sem, out_sem):
    flip = flip_ref[0]
    arriving = []
    for i in range(4):
        lanes = pl.ds(i * 512, 512)
        both = []
        for j, (source, target) in enumerate(((q_hbm, q_ref), (p_hbm, p_ref))):
            copy = pltpu.make_async_copy(
                source.at[:, :, lanes], target.at[:, :, lanes], in_sem.at[i, j]
            )
            copy.start()
            both.append(copy)
        arriving.append(both)
    leaving = []
    for pair in range(8):
        if pair % 2 == 0:
            for copy in arriving[pair // 2]:
                copy.wait()
        lanes = pl.ds(pair * 256, 256)
        for col in range(4):
            o_ref[pair * 8 + col] = q_ref[:, col, lanes]
            o_ref[pair * 8 + 4 + col] = p_ref[:, col, lanes]
        copy = pltpu.make_async_copy(
            o_ref.at[pl.ds(pair * 8, 8)],
            out_hbm.at[pl.ds(turned(pair, flip) * 8, 8)],
            out_sem.at[pair],
        )
        copy.start()
        leaving.append(copy)
    for copy in leaving:
        copy.wait()


def pack(flip, q_block, q_prev):
    hbm = pl.BlockSpec(memory_space=pltpu.HBM)
    return pl.pallas_call(
        pack_kernel,
        out_shape=f32(64, 8, 256),
        in_specs=[pl.BlockSpec(memory_space=pltpu.SMEM), hbm, hbm],
        out_specs=hbm,
        scratch_shapes=[
            pltpu.VMEM((8, 4, 2048), jnp.float32),
            pltpu.VMEM((8, 4, 2048), jnp.float32),
            pltpu.VMEM((64, 8, 256), jnp.float32),
            pltpu.SemaphoreType.DMA((4, 2)),
            pltpu.SemaphoreType.DMA((8,)),
        ],
        compiler_params=pltpu.CompilerParams(vmem_limit_bytes=VMEM_LIMIT),
    )(flip, q_block, q_prev)


def raw_kernel(q_ref, p_ref, gram_ref):
    total = jnp.zeros((8, 8), jnp.float32)
    for s in range(8):
        rows = jnp.concatenate([q_ref[s], p_ref[s]], axis=0)
        total += dot(rows, rows, NT)
    gram_ref[...] = jnp.zeros((8, 128), jnp.float32)
    gram_ref[:, 0:8] = total


def stats_kernel(pair_ref, s_ref, c_ref, out_ref, high_ref, low_ref):
    step = pl.program_id(0)
    row = lax.broadcasted_iota(jnp.int32, (128, 128), 0)
    col = lax.broadcasted_iota(jnp.int32, (128, 128), 1)
    big = jnp.float32(3.0e38)
    found = []
    for ref in (s_ref, c_ref):
        largest = jnp.max(jnp.abs(ref[0]), axis=0)
        largest = jnp.max(largest.reshape(16, 8, 128), axis=0)
        middle = ref[0, 2]
        top = jnp.max(jnp.where(row == col, middle, -big).reshape(16, 8, 128), axis=0)
        low = jnp.max(jnp.where(row == col, -middle, -big).reshape(16, 8, 128), axis=0)
        found += [largest, top, low]

    @pl.when(step == 0)
    def _():
        for i, v in enumerate(found):
            out_ref[i] = v

    @pl.when(step > 0)
    def _():
        for i, v in enumerate(found):
            out_ref[i] = jnp.maximum(out_ref[i], v)

    for half in range(2):

        @pl.when(step == pair_ref[0] * 2 + half)
        def _():
            for k in range(5):
                high, low = split(jnp.concatenate([s_ref[0, k].T, c_ref[0, k].T], axis=1))
                high_ref[half, k * 128 : k * 128 + 128] = high
                low_ref[half, k * 128 : k * 128 + 128] = low


def table_kernel(f_ref, rows_ref, turned_ref):
    high, low = split(f_ref[...])
    rows_ref[0:128], rows_ref[128:256] = high, low
    high, low = split(f_ref[...].T)
    turned_ref[:, 0:128], turned_ref[:, 128:256] = high, low


def forward_kernel(f_ref, r_ref, out_ref):
    high, low = split(r_ref[...].reshape(SECTORS, 256))
    both = fast(f_ref[...], high)
    out_ref[...] = (both[:128] + both[128:] + fast(f_ref[0:128], low)).reshape(8, 16, 256)


def apply_kernel(shift, left_ref, own_ref, right_ref, high_ref, low_ref, f_ref, k_ref, *out_refs):
    count = own_ref.shape[0]
    rows = count * 16
    own = own_ref[...].reshape(rows, 256)
    wide = jnp.concatenate(
        [left_ref[...].reshape(rows, 256), own, right_ref[...].reshape(rows, 256)], axis=1
    )
    high, low = split(wide)
    stacked = jnp.concatenate([high, low], axis=0)
    factor = f_ref[...][None]
    sigma, inverse = k_ref[0:1, :][None], k_ref[1:2, :][None]
    for half in range(2):
        lanes = slice(half * 128, half * 128 + 640)
        both = fast(stacked[:, lanes], high_ref[half])
        both = both[:rows] + both[rows:] + fast(high[:, lanes], low_ref[half])
        value = both[:, :128].reshape(count, 16, 128)
        value = value + factor * both[:, 128:].reshape(count, 16, 128)
        if shift:
            mine = own[:, half * 128 : half * 128 + 128].reshape(count, 16, 128)
            value = value - sigma * mine
        value = value * inverse
        size = count // len(out_refs)
        for i, ref in enumerate(out_refs):
            ref[:, :, half * 128 : half * 128 + 128] = value[i * size : (i + 1) * size]


def share_kernel(k0, k1, k2x, k2y, k3, raw_ref, out_ref):
    total = jnp.zeros((32, 32), jnp.float32)
    for r in range(16):
        rows = jnp.concatenate(
            [k0[:, r, :], k1[:, r, :], k2x[:, r, :], k2y[:, r, :], k3[:, r, :], jnp.zeros((4, 256), jnp.float32)],
            axis=0,
        )
        total += dot(rows, rows, NT)
    first = jnp.concatenate([raw_ref[:, 0:8], total[0:8, 8:32]], axis=1)
    packed = jnp.concatenate([first, total[8:16], total[16:24], total[24:32]], axis=1)
    group = lax.broadcasted_iota(jnp.int32, (16, 128), 1) // 32
    sets = (
        [k1[c] for c in range(4)],
        [k1[4 + c] for c in range(4)],
        [k2x[c] for c in range(4)],
        [k2y[c] for c in range(4)],
        [k3[c] for c in range(4)],
    )
    for m, columns in enumerate(sets):
        for half in range(2):
            tiles = [v[:, half * 128 : half * 128 + 128] for v in columns]
            for q in range(4):
                value = None
                for c in range(4):
                    by = (c - q) % 4 * 32
                    moved = pltpu.roll(tiles[c], by, 1) if by else tiles[c]
                    value = moved if value is None else jnp.where(group == c, moved, value)
                out_ref[half * 4 + q, m * 16 : m * 16 + 16] = value
    for d in range(8):
        out_ref[d, 80:88] = packed


def total_kernel(v_ref, out_ref):
    total = v_ref[0, 80:88]
    for d in range(1, 8):
        total += v_ref[d, 80:88]
    for d in range(32):
        out_ref[d] = total


def mixed(columns, rows):
    total = columns[0] * rows[0:1, :]
    for l in range(1, 4):
        total += columns[l] * rows[l : l + 1, :]
    return total


def products(a, b):
    return [jnp.sum(a * b[l : l + 1, :], axis=1, keepdims=True) for l in range(4)]


def square_of(columns):
    col = lax.broadcasted_iota(jnp.int32, (4, 4), 1)
    value = columns[0] + jnp.zeros((4, 4), jnp.float32)
    for l in range(1, 4):
        value = jnp.where(col == l, columns[l], value)
    return value


def solve_kernel(g_ref, b_ref, k_ref, v_ref, f_ref, image_ref, coef_ref, alpha_ref, beta_ref):
    lane = lax.broadcasted_iota(jnp.int32, (4, 128), 1)
    row = lax.broadcasted_iota(jnp.int32, (4, 128), 0)
    sigma, scale = k_ref[0:1, :], k_ref[2:3, :]
    packed = g_ref[0]
    for d in range(1, 32):
        packed += g_ref[d]
    narrow = lax.broadcasted_iota(jnp.int32, (8, 128), 1) < 32
    gram = jnp.concatenate(
        [
            jnp.where(narrow, packed if q == 0 else pltpu.roll(packed, 128 - 32 * q, 1), 0.0)
            for q in range(4)
        ],
        axis=0,
    )
    cur = (lane == row).astype(jnp.float32)
    prev = (lane == row + 4).astype(jnp.float32)
    cur_g, prev_g = gram[0:4], gram[4:8]
    coupling = [b_ref[:, l : l + 1] for l in range(4)]
    one_row = lax.broadcasted_iota(jnp.int32, (4, 1), 0)
    for step in range(3):
        moved = scale * pltpu.roll(jnp.where(lane < 20, cur, 0.0), 8, 1)
        moved += sigma * jnp.where(lane >= 8, cur, 0.0)
        w = moved - mixed(coupling, prev)
        w_g = dot(moved[:, 0:32], gram) - mixed(coupling, prev_g)
        across = products(w_g, cur)
        alpha_ref[step] = square_of(products(cur_g, w))
        r = w - mixed(across, cur)
        r_g = w_g - mixed(across, cur_g)
        square = products(r_g, r)
        pivots = jnp.zeros((4, 1), jnp.float32)
        for i in range(4):
            pivot = square[i][i : i + 1, :]
            pivots = jnp.where(one_row == i, pivot, pivots)
            if i < 3:
                times = jnp.where(one_row > i, square[i] / pivot, 0.0)
                r = r - times * r[i : i + 1, :]
                r_g = r_g - times * r_g[i : i + 1, :]
                square = [
                    v - times * v[i : i + 1, :] if l > i else v for l, v in enumerate(square)
                ]
        root = 1.0 / jnp.sqrt(pivots)
        upper = [jnp.where(one_row <= l, square[l] * root, 0.0) for l in range(4)]
        beta_ref[step] = square_of(upper)
        prev, prev_g, coupling = cur, cur_g, upper
        cur, cur_g = r * root, r_g * root
    coef_ref[...] = cur
    group = lane[0:1] // 32
    spread = (lane // 32 == row).astype(jnp.float32)
    weights = dot(cur, spread, TN)
    field = jnp.zeros((128, 128), jnp.float32)
    for m in range(5):
        tile = v_ref[:, m * 16 : m * 16 + 16].reshape(128, 128)
        for by in range(4):
            line = None
            for c in range(4):
                from_row = weights[8 + 4 * m + c : 9 + 4 * m + c, :]
                line = from_row if line is None else jnp.where(group == (c + by) % 4, from_row, line)
            field += line * (pltpu.roll(tile, 32 * by, 1) if by else tile)
    high, low = split(field)
    none = jnp.zeros((128, 128), jnp.bfloat16)
    right = jnp.concatenate(
        [jnp.concatenate([high, low], axis=1), jnp.concatenate([high, none], axis=1)], axis=0
    )
    both = fast(f_ref[...], right)
    image_ref[...] = (both[:, :128] + both[:, 128:]).reshape(64, 8, 128)


def base_kernel(flip_ref, q_ref, coef_ref, out_ref):
    flip = flip_ref[0]
    coef = coef_ref[...]
    scalars = [
        [coef[c : c + 1, k : k + 1] + jnp.zeros((8, 256), jnp.float32) for k in range(8)]
        for c in range(4)
    ]
    for pair in range(8):
        place = turned(pair, flip) * 8
        tiles = [q_ref[place + k] for k in range(8)]
        for c in range(4):
            total = scalars[c][0] * tiles[0]
            for k in range(1, 8):
                total += scalars[c][k] * tiles[k]
            out_ref[pair, c] = total


def last_kernel(flip_ref, r_ref, base_ref, out_ref):
    flip = flip_ref[0]
    group = lax.broadcasted_iota(jnp.int32, (8, 128), 1) // 32
    for pair in range(8):
        place = turned(pair, flip) * 8
        for half in range(2):
            tiles = [r_ref[place + half * 4 + q] for q in range(4)]
            for c in range(4):
                value = None
                for q in range(4):
                    by = (q - c) % 4 * 32
                    moved = pltpu.roll(tiles[q], by, 1) if by else tiles[q]
                    value = moved if value is None else jnp.where(group == q, moved, value)
                value += base_ref[pair, c, :, half * 128 : half * 128 + 128]
                out_ref[:, c, pl.ds(pair * 256 + half * 128, 128)] = value


def table(assign):
    harmonic = jnp.repeat(assign, 2)
    parity = jnp.arange(harmonic.shape[0], dtype=jnp.int32) % 2
    sectors = jnp.arange(SECTORS, dtype=jnp.int32)
    phases = (harmonic[:, None] * sectors[None, :] + 128 * parity[:, None]) % SECTORS
    weights = jnp.where(harmonic == 0, math.sqrt(1.0 / SECTORS), math.sqrt(2.0 / SECTORS))
    weights = jnp.where((harmonic == 0) & (parity == 1), 0.0, weights).astype(jnp.float32)
    return jnp.cos(2.0 * math.pi / SECTORS * phases.astype(jnp.float32)) * weights[:, None]


def ring_place(pair):
    slab, at = pair // 8 % 4, pair % 8
    return (at if slab % 2 == 0 else 7 - at) * 4 + slab


def beside(value):
    after = [(ring_place(i), ring_place(i + 1)) for i in range(32)]
    before = [(j, i) for i, j in after]
    return lax.ppermute(value, RING, after), lax.ppermute(value, RING, before)


def highest(value, step):
    return jnp.maximum(value, lax.ppermute(value, "xs", [(i, i ^ step) for i in range(4)]))


def per_device(q_block, q_prev, b_prev, stiff_blocks, couple_blocks, block_cols, assign):
    flip = (lax.axis_index("xs") % 2).astype(jnp.int32).reshape(1)
    pair = turned(lax.axis_index("z"), flip)
    group = lax.axis_index("y") * 2 + lax.axis_index("core")

    packed = pack(flip, q_block, q_prev)
    received = lax.all_to_all(packed, SEC, 0, 0, tiled=True)

    forward, inverse = call(table_kernel, (bf16(256, 512), bf16(512, 256)), table(assign))
    factors = jnp.cos(2.0 * math.pi / SECTORS * assign.astype(jnp.float32))
    mine = lax.dynamic_slice_in_dim(factors, group * 8, 8)
    factor = jnp.broadcast_to(jnp.repeat(mine, 2)[:, None], (16, 128))
    raw = call(raw_kernel, f32(8, 128), q_block, q_prev)
    found, own_high, own_low = pl.pallas_call(
        stats_kernel,
        out_shape=(f32(6, 8, 128), bf16(2, 640, 256), bf16(2, 640, 256)),
        grid_spec=pltpu.PrefetchScalarGridSpec(
            num_scalar_prefetch=1,
            grid=(16,),
            in_specs=[pl.BlockSpec((1, 5, 128, 128), lambda i, p: (i, 0, 0, 0))] * 2,
            out_specs=(
                pl.BlockSpec((6, 8, 128), lambda i, p: (0, 0, 0)),
                pl.BlockSpec((2, 640, 256), lambda i, p: (0, 0, 0)),
                pl.BlockSpec((2, 640, 256), lambda i, p: (0, 0, 0)),
            ),
        ),
        compiler_params=pltpu.CompilerParams(vmem_limit_bytes=VMEM_LIMIT),
    )(pair, stiff_blocks, couple_blocks)
    found = jnp.broadcast_to(jnp.max(found, axis=(1, 2))[:, None], (6, 128))
    found = highest(highest(found, 1), 2)
    sigma = 0.5 * (found[1] - found[2]) + jnp.mean(factors) * (0.5 * (found[4] - found[5]))
    scale = found[0] + found[3]
    scale = jnp.where(scale > 0, scale, 1.0)
    scales = jnp.stack([sigma, 1.0 / scale, scale] + [scale] * 5)

    spectrum = call(forward_kernel, f32(8, 16, 256), forward, received)
    k0 = lax.all_to_all(spectrum, GROUP, 0, 0, tiled=True)

    def operator(value, shift, out):
        left, right = beside(value)
        return call(
            lambda *refs: apply_kernel(shift, *refs), out, left, value, right, own_high, own_low, factor, scales
        )

    (k1,) = operator(k0, False, (f32(8, 16, 256),))
    k2x, k2y = operator(k1, True, (f32(4, 16, 256), f32(4, 16, 256)))
    (k3,) = operator(k2x, True, (f32(4, 16, 256),))

    shares = call(share_kernel, f32(8, 88, 128), k0, k1, k2x, k2y, k3, raw)
    vectors = lax.all_to_all(shares, GROUP, 0, 0, tiled=True)
    grams = lax.all_to_all(call(total_kernel, f32(32, 8, 128), vectors), RING, 0, 0, tiled=True)
    image, coef, alphas, betas = call(
        solve_kernel,
        (f32(64, 8, 128), f32(4, 128), f32(3, 4, 4), f32(3, 4, 4)),
        grams, b_prev, scales, vectors, inverse,
    )
    back = lax.all_to_all(image, SEC, 0, 0, tiled=True)
    base = call(base_kernel, f32(8, 4, 8, 256), packed, coef, scalar=flip)
    out = call(last_kernel, f32(8, 4, 2048), back, base, scalar=flip)
    return out, alphas, betas


def solution(mesh):
    fine = Mesh(mesh.devices.reshape(8, 4, 2, 4), ("z", "y", "core", "xs"))
    in_specs = (
        P(SEC, None, "xs"),
        P(SEC, None, "xs"),
        P(),
        P("xs", None, None, None),
        P("xs", None, None, None),
        P("xs", None),
        P(),
    )
    out_specs = (P(SEC, None, "xs"), P(), P())
    return jax.shard_map(
        per_device, mesh=fine, in_specs=in_specs, out_specs=out_specs, check_vma=False
    )
```

```python
import math

import jax
import jax.numpy as jnp
from jax import lax
from jax.experimental import pallas as pl
from jax.experimental.pallas import tpu as pltpu
from jax.sharding import Mesh
from jax.sharding import PartitionSpec as P

HI = lax.Precision.HIGHEST
SEC = ("z", "y", "core")
GROUP = ("y", "core")
RING = ("z", "xs")
SECTORS = 512
NT = (((1,), (1,)), ((), ()))
TN = (((0,), (0,)), ((), ()))
VMEM_LIMIT = 32 * 1024 * 1024
PACK_LIMIT = 60 * 1024 * 1024


def f32(*shape):
    return jax.ShapeDtypeStruct(shape, jnp.float32)


def dot(a, b, dims=(((1,), (0,)), ((), ()))):
    return lax.dot_general(a, b, dims, precision=HI, preferred_element_type=jnp.float32)


def bf16(*shape):
    return jax.ShapeDtypeStruct(shape, jnp.bfloat16)


def split(value):
    high = value.astype(jnp.bfloat16)
    return high, (value - high.astype(jnp.float32)).astype(jnp.bfloat16)


def fast(a, b):
    return lax.dot_general(a, b, (((1,), (0,)), ((), ())), preferred_element_type=jnp.float32)


def call(kernel, out, *args, scalar=None, **kw):
    whole = pl.BlockSpec(memory_space=pltpu.VMEM)
    specs = [whole] * len(args)
    if scalar is not None:
        specs = [pl.BlockSpec(memory_space=pltpu.SMEM)] + specs
        args = (scalar,) + args
    return pl.pallas_call(
        kernel,
        out_shape=out,
        in_specs=specs,
        out_specs=jax.tree.map(lambda _: whole, out),
        compiler_params=pltpu.CompilerParams(vmem_limit_bytes=VMEM_LIMIT),
        **kw,
    )(*args)


def turned(pair, flip):
    return pair + flip * (7 - 2 * pair)


def pack_kernel(flip_ref, q_hbm, p_hbm, out_hbm, q_ref, p_ref, o_ref, in_sem, out_sem):
    flip = flip_ref[0]
    arriving = []
    for i in range(4):
        lanes = pl.ds(i * 512, 512)
        both = []
        for j, (source, target) in enumerate(((q_hbm, q_ref), (p_hbm, p_ref))):
            copy = pltpu.make_async_copy(
                source.at[:, :, lanes], target.at[:, :, lanes], in_sem.at[i, j]
            )
            copy.start()
            both.append(copy)
        arriving.append(both)
    leaving = []
    for pair in range(8):
        if pair % 2 == 0:
            for copy in arriving[pair // 2]:
                copy.wait()
        lanes = pl.ds(pair * 256, 256)
        for col in range(4):
            o_ref[pair * 8 + col] = q_ref[:, col, lanes]
            o_ref[pair * 8 + 4 + col] = p_ref[:, col, lanes]
        copy = pltpu.make_async_copy(
            o_ref.at[pl.ds(pair * 8, 8)],
            out_hbm.at[pl.ds(turned(pair, flip) * 8, 8)],
            out_sem.at[pair],
        )
        copy.start()
        leaving.append(copy)
    for copy in leaving:
        copy.wait()


def pack(flip, q_block, q_prev):
    hbm = pl.BlockSpec(memory_space=pltpu.HBM)
    return pl.pallas_call(
        pack_kernel,
        out_shape=f32(64, 8, 256),
        in_specs=[pl.BlockSpec(memory_space=pltpu.SMEM), hbm, hbm],
        out_specs=hbm,
        scratch_shapes=[
            pltpu.VMEM((8, 4, 2048), jnp.float32),
            pltpu.VMEM((8, 4, 2048), jnp.float32),
            pltpu.VMEM((64, 8, 256), jnp.float32),
            pltpu.SemaphoreType.DMA((4, 2)),
            pltpu.SemaphoreType.DMA((8,)),
        ],
        compiler_params=pltpu.CompilerParams(vmem_limit_bytes=PACK_LIMIT),
    )(flip, q_block, q_prev)


def raw_kernel(q_ref, p_ref, gram_ref):
    total = jnp.zeros((8, 8), jnp.float32)
    for s in range(8):
        rows = jnp.concatenate([q_ref[s], p_ref[s]], axis=0)
        total += dot(rows, rows, NT)
    gram_ref[...] = jnp.zeros((8, 128), jnp.float32)
    gram_ref[:, 0:8] = total


def rest_kernel(k0_ref, raw_ref, b_ref, k_ref, out_ref):
    inside = jnp.zeros((8, 8), jnp.float32)
    for r in range(16):
        rows = k0_ref[:, r, :]
        inside += dot(rows, rows, NT)
    outside = raw_ref[:, 0:8] - inside
    row = lax.broadcasted_iota(jnp.int32, (4, 4), 0)
    col = lax.broadcasted_iota(jnp.int32, (4, 4), 1)
    none = jnp.zeros((4, 4), jnp.float32)
    change = jnp.concatenate(
        [
            jnp.concatenate([(row == col).astype(jnp.float32), none], axis=1),
            jnp.concatenate([none, -k_ref[1:2, 0:1] * b_ref[...]], axis=1),
        ],
        axis=0,
    )
    out_ref[...] = jnp.zeros((8, 128), jnp.float32)
    out_ref[:, 0:8] = dot(dot(change, outside), change, NT)


def stats_kernel(pair_ref, s_ref, c_ref, out_ref, high_ref, low_ref):
    step = pl.program_id(0)
    row = lax.broadcasted_iota(jnp.int32, (128, 128), 0)
    col = lax.broadcasted_iota(jnp.int32, (128, 128), 1)
    big = jnp.float32(3.0e38)
    found = []
    for ref in (s_ref, c_ref):
        largest = jnp.max(jnp.abs(ref[0]), axis=0)
        largest = jnp.max(largest.reshape(16, 8, 128), axis=0)
        middle = ref[0, 2]
        top = jnp.max(jnp.where(row == col, middle, -big).reshape(16, 8, 128), axis=0)
        low = jnp.max(jnp.where(row == col, -middle, -big).reshape(16, 8, 128), axis=0)
        found += [largest, top, low]

    @pl.when(step == 0)
    def _():
        for i, v in enumerate(found):
            out_ref[i] = v

    @pl.when(step > 0)
    def _():
        for i, v in enumerate(found):
            out_ref[i] = jnp.maximum(out_ref[i], v)

    for half in range(2):

        @pl.when(step == pair_ref[0] * 2 + half)
        def _():
            for k in range(5):
                high, low = split(jnp.concatenate([s_ref[0, k].T, c_ref[0, k].T], axis=1))
                high_ref[half, k * 128 : k * 128 + 128] = high
                low_ref[half, k * 128 : k * 128 + 128] = low


def table_kernel(f_ref, rows_ref, turned_ref):
    high, low = split(f_ref[...])
    rows_ref[0:128], rows_ref[128:256] = high, low
    high, low = split(f_ref[...].T)
    turned_ref[:, 0:128], turned_ref[:, 128:256] = high, low


def forward_kernel(f_ref, r_ref, out_ref):
    high, low = split(r_ref[...].reshape(SECTORS, 256))
    both = fast(f_ref[...], high)
    out_ref[...] = (both[:128] + both[128:] + fast(f_ref[0:128], low)).reshape(8, 16, 256)


def apply_kernel(stage, left_ref, own_ref, right_ref, high_ref, low_ref, f_ref, k_ref, *refs):
    count = left_ref.shape[0]
    rows = count * 16
    wide = jnp.concatenate(
        [ref[0:count].reshape(rows, 256) for ref in (left_ref, own_ref, right_ref)], axis=1
    )
    high, low = split(wide)
    stacked = jnp.concatenate([high, low], axis=0)
    factor = f_ref[...][None]
    sigma, inverse = k_ref[0:1, :][None], k_ref[1:2, :][None]
    for half in range(2):
        lanes = slice(half * 128, half * 128 + 640)
        both = fast(stacked[:, lanes], high_ref[half])
        both = both[:rows] + both[rows:] + fast(high[:, lanes], low_ref[half])
        value = both[:, :128].reshape(count, 16, 128)
        value = value + factor * both[:, 128:].reshape(count, 16, 128)
        here = slice(half * 128, half * 128 + 128)
        if stage == 1:
            b_ref, out_ref = refs
            value = value * inverse
            out_ref[0:4, :, here] = value
            for i in range(4):
                taken = b_ref[i, 0] * own_ref[4, :, here]
                for l in range(1, 4):
                    taken += b_ref[i, l] * own_ref[4 + l, :, here]
                out_ref[4 + i, :, here] = value[i] - inverse[0] * taken
        elif stage == 2:
            x_ref, w_ref = refs
            x_ref[:, :, here] = (value[0:4] - sigma * own_ref[0:4, :, here]) * inverse
            w_ref[:, :, here] = value[4:8] * inverse
        else:
            (out_ref,) = refs
            out_ref[:, :, here] = (value - sigma * own_ref[:, :, here]) * inverse


def share_kernel(k0, s1, k2x, k2w, k3, rest_ref, out_ref):
    total = jnp.zeros((24, 24), jnp.float32)
    for r in range(16):
        rows = jnp.concatenate(
            [k0[0:4, r, :], s1[4:8, r, :], s1[0:4, r, :], k2w[:, r, :], k2x[:, r, :], k3[:, r, :]],
            axis=0,
        )
        total += dot(rows, rows, NT)
    first = jnp.concatenate([total[0:8, 0:8] + rest_ref[:, 0:8], total[0:8, 8:24]], axis=1)
    pad = jnp.zeros((8, 8), jnp.float32)
    packed = jnp.concatenate(
        [first, pad, total[8:16], pad, total[16:24], pad, jnp.zeros((8, 32), jnp.float32)], axis=1
    )
    group = lax.broadcasted_iota(jnp.int32, (16, 128), 1) // 32
    sets = tuple([ref[c] for c in range(4)] for ref in (s1, k2w, k2x, k3))
    for m, columns in enumerate(sets):
        for half in range(2):
            tiles = [v[:, half * 128 : half * 128 + 128] for v in columns]
            for q in range(4):
                value = None
                for c in range(4):
                    by = (c - q) % 4 * 32
                    moved = pltpu.roll(tiles[c], by, 1) if by else tiles[c]
                    value = moved if value is None else jnp.where(group == c, moved, value)
                out_ref[half * 4 + q, m * 16 : m * 16 + 16] = value
    for d in range(8):
        out_ref[d, 64:72] = packed


def total_kernel(v_ref, out_ref):
    total = v_ref[0, 64:72]
    for d in range(1, 8):
        total += v_ref[d, 64:72]
    for d in range(32):
        out_ref[d] = total


def mixed(columns, rows):
    total = columns[0] * rows[0:1, :]
    for l in range(1, 4):
        total += columns[l] * rows[l : l + 1, :]
    return total


def products(a, b):
    return [jnp.sum(a * b[l : l + 1, :], axis=1, keepdims=True) for l in range(4)]


def square_of(columns):
    col = lax.broadcasted_iota(jnp.int32, (4, 4), 1)
    value = columns[0] + jnp.zeros((4, 4), jnp.float32)
    for l in range(1, 4):
        value = jnp.where(col == l, columns[l], value)
    return value


def solve_kernel(g_ref, b_ref, k_ref, v_ref, f_ref, image_ref, coef_ref, alpha_ref, beta_ref):
    lane = lax.broadcasted_iota(jnp.int32, (4, 128), 1)
    row = lax.broadcasted_iota(jnp.int32, (4, 128), 0)
    sigma, scale = k_ref[0:1, :], k_ref[2:3, :]
    packed = g_ref[0]
    for d in range(1, 32):
        packed += g_ref[d]
    narrow = lax.broadcasted_iota(jnp.int32, (8, 128), 1) < 32
    gram = jnp.concatenate(
        [
            jnp.where(narrow, packed if q == 0 else pltpu.roll(packed, 128 - 32 * q, 1), 0.0)
            for q in range(3)
        ],
        axis=0,
    )
    cur = (lane == row).astype(jnp.float32)
    cur_g = gram[0:4]
    prev = prev_g = coupling = None
    one_row = lax.broadcasted_iota(jnp.int32, (4, 1), 0)
    for step in range(3):
        if step == 0:
            w = scale * (lane == row + 4).astype(jnp.float32)
            w_g = scale * gram[4:8]
        else:
            moved = scale * pltpu.roll(jnp.where(lane < 16, cur, 0.0), 8, 1)
            moved += sigma * jnp.where(lane >= 8, cur, 0.0)
            w = moved - mixed(coupling, prev)
            w_g = dot(moved[:, 0:24], gram) - mixed(coupling, prev_g)
        across = products(w_g, cur)
        alpha_ref[step] = square_of(products(cur_g, w))
        r = w - mixed(across, cur)
        r_g = w_g - mixed(across, cur_g)
        square = products(r_g, r)
        pivots = jnp.zeros((4, 1), jnp.float32)
        for i in range(4):
            pivot = square[i][i : i + 1, :]
            pivots = jnp.where(one_row == i, pivot, pivots)
            if i < 3:
                times = jnp.where(one_row > i, square[i] / pivot, 0.0)
                r = r - times * r[i : i + 1, :]
                r_g = r_g - times * r_g[i : i + 1, :]
                square = [
                    v - times * v[i : i + 1, :] if l > i else v for l, v in enumerate(square)
                ]
        root = 1.0 / jnp.sqrt(pivots)
        upper = [jnp.where(one_row <= l, square[l] * root, 0.0) for l in range(4)]
        beta_ref[step] = square_of(upper)
        prev, prev_g, coupling = cur, cur_g, upper
        cur, cur_g = r * root, r_g * root
    coef_ref[...] = cur
    behind = cur[:, 4:5] * b_ref[0:1, :]
    for l in range(1, 4):
        behind += cur[:, 4 + l : 5 + l] * b_ref[l : l + 1, :]
    coef_ref[:, 4:8] = -k_ref[1:2, 0:1] * behind
    cur += pltpu.roll(jnp.where((lane >= 4) & (lane < 8), cur, 0.0), 4, 1)
    group = lane[0:1] // 32
    spread = (lane // 32 == row).astype(jnp.float32)
    weights = dot(cur, spread, TN)
    field = jnp.zeros((128, 128), jnp.float32)
    for m in range(4):
        tile = v_ref[:, m * 16 : m * 16 + 16].reshape(128, 128)
        for by in range(4):
            line = None
            for c in range(4):
                from_row = weights[8 + 4 * m + c : 9 + 4 * m + c, :]
                line = from_row if line is None else jnp.where(group == (c + by) % 4, from_row, line)
            field += line * (pltpu.roll(tile, 32 * by, 1) if by else tile)
    high, low = split(field)
    none = jnp.zeros((128, 128), jnp.bfloat16)
    right = jnp.concatenate(
        [jnp.concatenate([high, low], axis=1), jnp.concatenate([high, none], axis=1)], axis=0
    )
    both = fast(f_ref[...], right)
    image_ref[...] = (both[:, :128] + both[:, 128:]).reshape(64, 8, 128)


def base_kernel(flip_ref, q_ref, coef_ref, out_ref):
    flip = flip_ref[0]
    coef = coef_ref[...]
    scalars = [
        [coef[c : c + 1, k : k + 1] + jnp.zeros((8, 256), jnp.float32) for k in range(8)]
        for c in range(4)
    ]
    for pair in range(8):
        place = turned(pair, flip) * 8
        tiles = [q_ref[place + k] for k in range(8)]
        for c in range(4):
            total = scalars[c][0] * tiles[0]
            for k in range(1, 8):
                total += scalars[c][k] * tiles[k]
            out_ref[pair, c] = total


def last_kernel(flip_ref, r_ref, base_ref, out_ref):
    flip = flip_ref[0]
    group = lax.broadcasted_iota(jnp.int32, (8, 128), 1) // 32
    for pair in range(8):
        place = turned(pair, flip) * 8
        for half in range(2):
            tiles = [r_ref[place + half * 4 + q] for q in range(4)]
            for c in range(4):
                value = None
                for q in range(4):
                    by = (q - c) % 4 * 32
                    moved = pltpu.roll(tiles[q], by, 1) if by else tiles[q]
                    value = moved if value is None else jnp.where(group == q, moved, value)
                value += base_ref[pair, c, :, half * 128 : half * 128 + 128]
                out_ref[:, c, pl.ds(pair * 256 + half * 128, 128)] = value


def table(assign):
    harmonic = jnp.repeat(assign, 2)
    parity = jnp.arange(harmonic.shape[0], dtype=jnp.int32) % 2
    sectors = jnp.arange(SECTORS, dtype=jnp.int32)
    phases = (harmonic[:, None] * sectors[None, :] + 128 * parity[:, None]) % SECTORS
    weights = jnp.where(harmonic == 0, math.sqrt(1.0 / SECTORS), math.sqrt(2.0 / SECTORS))
    weights = jnp.where((harmonic == 0) & (parity == 1), 0.0, weights).astype(jnp.float32)
    return jnp.cos(2.0 * math.pi / SECTORS * phases.astype(jnp.float32)) * weights[:, None]


def ring_place(pair):
    slab, at = pair // 8 % 4, pair % 8
    return (at if slab % 2 == 0 else 7 - at) * 4 + slab


def beside(value):
    after = [(ring_place(i), ring_place(i + 1)) for i in range(32)]
    before = [(j, i) for i, j in after]
    return lax.ppermute(value, RING, after), lax.ppermute(value, RING, before)


def highest(value, step):
    return jnp.maximum(value, lax.ppermute(value, "xs", [(i, i ^ step) for i in range(4)]))


def per_device(q_block, q_prev, b_prev, stiff_blocks, couple_blocks, block_cols, assign):
    flip = (lax.axis_index("xs") % 2).astype(jnp.int32).reshape(1)
    pair = turned(lax.axis_index("z"), flip)
    group = lax.axis_index("y") * 2 + lax.axis_index("core")

    packed = pack(flip, q_block, q_prev)
    received = lax.all_to_all(packed, SEC, 0, 0, tiled=True)

    forward, inverse = call(table_kernel, (bf16(256, 512), bf16(512, 256)), table(assign))
    factors = jnp.cos(2.0 * math.pi / SECTORS * assign.astype(jnp.float32))
    mine = lax.dynamic_slice_in_dim(factors, group * 8, 8)
    factor = jnp.broadcast_to(jnp.repeat(mine, 2)[:, None], (16, 128))
    raw = call(raw_kernel, f32(8, 128), q_block, q_prev)
    found, own_high, own_low = pl.pallas_call(
        stats_kernel,
        out_shape=(f32(6, 8, 128), bf16(2, 640, 256), bf16(2, 640, 256)),
        grid_spec=pltpu.PrefetchScalarGridSpec(
            num_scalar_prefetch=1,
            grid=(16,),
            in_specs=[pl.BlockSpec((1, 5, 128, 128), lambda i, p: (i, 0, 0, 0))] * 2,
            out_specs=(
                pl.BlockSpec((6, 8, 128), lambda i, p: (0, 0, 0)),
                pl.BlockSpec((2, 640, 256), lambda i, p: (0, 0, 0)),
                pl.BlockSpec((2, 640, 256), lambda i, p: (0, 0, 0)),
            ),
        ),
        compiler_params=pltpu.CompilerParams(vmem_limit_bytes=VMEM_LIMIT),
    )(pair, stiff_blocks, couple_blocks)
    found = jnp.broadcast_to(jnp.max(found, axis=(1, 2))[:, None], (6, 128))
    found = highest(highest(found, 1), 2)
    sigma = 0.5 * (found[1] - found[2]) + jnp.mean(factors) * (0.5 * (found[4] - found[5]))
    scale = found[0] + found[3]
    scale = jnp.where(scale > 0, scale, 1.0)
    scales = jnp.stack([sigma, 1.0 / scale, scale] + [scale] * 5)

    spectrum = call(forward_kernel, f32(8, 16, 256), forward, received)
    k0 = lax.all_to_all(spectrum, GROUP, 0, 0, tiled=True)

    def operator(stage, sent, value, out, *more):
        left, right = beside(sent)
        specs = [pl.BlockSpec(memory_space=pltpu.VMEM)] * 7
        specs += [pl.BlockSpec(memory_space=pltpu.SMEM)] * len(more)
        return pl.pallas_call(
            lambda *refs: apply_kernel(stage, *refs),
            out_shape=out,
            in_specs=specs,
            out_specs=jax.tree.map(lambda _: specs[0], out),
            compiler_params=pltpu.CompilerParams(vmem_limit_bytes=VMEM_LIMIT),
        )(left, value, right, own_high, own_low, factor, scales, *more)

    s1 = operator(1, k0[0:4], k0, f32(8, 16, 256), b_prev)
    rest = call(rest_kernel, f32(8, 128), k0, raw, b_prev, scales)
    k2x, k2w = operator(2, s1, s1, (f32(4, 16, 256), f32(4, 16, 256)))
    k3 = operator(3, k2w, k2w, f32(4, 16, 256))

    shares = call(share_kernel, f32(8, 72, 128), k0, s1, k2x, k2w, k3, rest)
    vectors = lax.all_to_all(shares, GROUP, 0, 0, tiled=True)
    grams = lax.all_to_all(call(total_kernel, f32(32, 8, 128), vectors), RING, 0, 0, tiled=True)
    image, coef, alphas, betas = call(
        solve_kernel,
        (f32(64, 8, 128), f32(4, 128), f32(3, 4, 4), f32(3, 4, 4)),
        grams, b_prev, scales, vectors, inverse,
    )
    back = lax.all_to_all(image, SEC, 0, 0, tiled=True)
    base = call(base_kernel, f32(8, 4, 8, 256), packed, coef, scalar=flip)
    out = call(last_kernel, f32(8, 4, 2048), back, base, scalar=flip)
    return out, alphas, betas


def solution(mesh):
    fine = Mesh(mesh.devices.reshape(8, 4, 2, 4), ("z", "y", "core", "xs"))
    in_specs = (
        P(SEC, None, "xs"),
        P(SEC, None, "xs"),
        P(),
        P("xs", None, None, None),
        P("xs", None, None, None),
        P("xs", None),
        P(),
    )
    out_specs = (P(SEC, None, "xs"), P(), P())
    return jax.shard_map(
        per_device, mesh=fine, in_specs=in_specs, out_specs=out_specs, check_vma=False
    )
```

```python
import math

import jax
import jax.numpy as jnp
from jax import lax
from jax.experimental import pallas as pl
from jax.experimental.pallas import tpu as pltpu
from jax.sharding import Mesh
from jax.sharding import PartitionSpec as P

HI = lax.Precision.HIGHEST
SEC = ("z", "y", "core")
GROUP = ("y", "core")
RING = ("z", "xs")
SECTORS = 512
NT = (((1,), (1,)), ((), ()))
TN = (((0,), (0,)), ((), ()))
VMEM_LIMIT = 32 * 1024 * 1024
PACK_LIMIT = 60 * 1024 * 1024


def f32(*shape):
    return jax.ShapeDtypeStruct(shape, jnp.float32)


def dot(a, b, dims=(((1,), (0,)), ((), ()))):
    return lax.dot_general(a, b, dims, precision=HI, preferred_element_type=jnp.float32)


def bf16(*shape):
    return jax.ShapeDtypeStruct(shape, jnp.bfloat16)


def split(value):
    high = value.astype(jnp.bfloat16)
    return high, (value - high.astype(jnp.float32)).astype(jnp.bfloat16)


def fast(a, b):
    return lax.dot_general(a, b, (((1,), (0,)), ((), ())), preferred_element_type=jnp.float32)


def call(kernel, out, *args):
    whole = pl.BlockSpec(memory_space=pltpu.VMEM)
    return pl.pallas_call(
        kernel,
        out_shape=out,
        in_specs=[whole] * len(args),
        out_specs=jax.tree.map(lambda _: whole, out),
        compiler_params=pltpu.CompilerParams(vmem_limit_bytes=VMEM_LIMIT),
    )(*args)


def odd_slab():
    return lax.rem(lax.axis_index("xs"), 2)


def turned(pair, flip):
    return pair + flip * (7 - 2 * pair)


def pack_kernel(q_hbm, p_hbm, out_hbm, q_ref, p_ref, o_ref, in_sem, out_sem):
    flip = odd_slab()
    arriving = []
    for i in range(4):
        lanes = pl.ds(i * 512, 512)
        both = []
        for j, (source, target) in enumerate(((q_hbm, q_ref), (p_hbm, p_ref))):
            copy = pltpu.make_async_copy(
                source.at[:, :, lanes], target.at[:, :, lanes], in_sem.at[i, j]
            )
            copy.start()
            both.append(copy)
        arriving.append(both)
    leaving = []
    for pair in range(8):
        if pair % 2 == 0:
            for copy in arriving[pair // 2]:
                copy.wait()
        lanes = pl.ds(pair * 256, 256)
        for col in range(4):
            o_ref[pair * 8 + col] = q_ref[:, col, lanes]
            o_ref[pair * 8 + 4 + col] = p_ref[:, col, lanes]
        copy = pltpu.make_async_copy(
            o_ref.at[pl.ds(pair * 8, 8)],
            out_hbm.at[pl.ds(turned(pair, flip) * 8, 8)],
            out_sem.at[pair],
        )
        copy.start()
        leaving.append(copy)
    for copy in leaving:
        copy.wait()


def pack(q_block, q_prev):
    hbm = pl.BlockSpec(memory_space=pltpu.HBM)
    return pl.pallas_call(
        pack_kernel,
        out_shape=f32(64, 8, 256),
        in_specs=[hbm, hbm],
        out_specs=hbm,
        scratch_shapes=[
            pltpu.VMEM((8, 4, 2048), jnp.float32),
            pltpu.VMEM((8, 4, 2048), jnp.float32),
            pltpu.VMEM((64, 8, 256), jnp.float32),
            pltpu.SemaphoreType.DMA((4, 2)),
            pltpu.SemaphoreType.DMA((8,)),
        ],
        compiler_params=pltpu.CompilerParams(vmem_limit_bytes=PACK_LIMIT),
    )(q_block, q_prev)


def raw_kernel(q_ref, p_ref, gram_ref):
    total = jnp.zeros((8, 8), jnp.float32)
    for s in range(8):
        rows = jnp.concatenate([q_ref[s], p_ref[s]], axis=0)
        total += dot(rows, rows, NT)
    gram_ref[...] = jnp.zeros((8, 128), jnp.float32)
    gram_ref[:, 0:8] = total


def rest_kernel(k0_ref, raw_ref, b_ref, k_ref, out_ref):
    inside = jnp.zeros((8, 8), jnp.float32)
    for r in range(16):
        rows = k0_ref[:, r, :]
        inside += dot(rows, rows, NT)
    outside = raw_ref[:, 0:8] - inside
    row = lax.broadcasted_iota(jnp.int32, (4, 4), 0)
    col = lax.broadcasted_iota(jnp.int32, (4, 4), 1)
    none = jnp.zeros((4, 4), jnp.float32)
    change = jnp.concatenate(
        [
            jnp.concatenate([(row == col).astype(jnp.float32), none], axis=1),
            jnp.concatenate([none, -k_ref[1:2, 0:1] * b_ref[...]], axis=1),
        ],
        axis=0,
    )
    out_ref[...] = jnp.zeros((8, 128), jnp.float32)
    out_ref[:, 0:8] = dot(dot(change, outside), change, NT)


def stats_kernel(pair_ref, s_ref, c_ref, out_ref, high_ref, low_ref, best_ref):
    step = pl.program_id(0)
    row = lax.broadcasted_iota(jnp.int32, (128, 128), 0)
    col = lax.broadcasted_iota(jnp.int32, (128, 128), 1)
    big = jnp.float32(3.0e38)
    found = []
    for ref in (s_ref, c_ref):
        largest = jnp.max(jnp.abs(ref[0]), axis=0)
        largest = jnp.max(largest.reshape(16, 8, 128), axis=0)
        middle = ref[0, 2]
        top = jnp.max(jnp.where(row == col, middle, -big).reshape(16, 8, 128), axis=0)
        low = jnp.max(jnp.where(row == col, -middle, -big).reshape(16, 8, 128), axis=0)
        found += [largest, top, low]

    @pl.when(step == 0)
    def _():
        for i, v in enumerate(found):
            best_ref[i] = v

    @pl.when(step > 0)
    def _():
        for i, v in enumerate(found):
            best_ref[i] = jnp.maximum(best_ref[i], v)

    @pl.when(step == 15)
    def _():
        out_ref[...] = jnp.zeros((8, 128), jnp.float32)
        for i in range(6):
            best = jnp.max(best_ref[i], axis=(0, 1), keepdims=True)
            out_ref[i : i + 1] = best + jnp.zeros((1, 128), jnp.float32)

    for half in range(2):

        @pl.when(step == pair_ref[0] * 2 + half)
        def _():
            for k in range(5):
                high, low = split(jnp.concatenate([s_ref[0, k].T, c_ref[0, k].T], axis=1))
                high_ref[half, k * 128 : k * 128 + 128] = high
                low_ref[half, k * 128 : k * 128 + 128] = low


def table_kernel(f_ref, rows_ref, turned_ref):
    high, low = split(f_ref[...])
    rows_ref[0:128], rows_ref[128:256] = high, low
    high, low = split(f_ref[...].T)
    turned_ref[:, 0:128], turned_ref[:, 128:256] = high, low


def forward_kernel(f_ref, r_ref, *refs):
    out_ref = refs[-1]
    high, low = split(r_ref[...].reshape(SECTORS, 256))
    both = fast(f_ref[...], high)
    out_ref[...] = (both[:128] + both[128:] + fast(f_ref[0:128], low)).reshape(8, 16, 256)


def apply_kernel(stage, left_ref, own_ref, right_ref, high_ref, low_ref, f_ref, k_ref, *refs):
    count = left_ref.shape[0]
    rows = count * 16
    wide = jnp.concatenate(
        [ref[0:count].reshape(rows, 256) for ref in (left_ref, own_ref, right_ref)], axis=1
    )
    high, low = split(wide)
    stacked = jnp.concatenate([high, low], axis=0)
    factor = f_ref[...][None]
    sigma, inverse = k_ref[0:1, :][None], k_ref[1:2, :][None]
    for half in range(2):
        lanes = slice(half * 128, half * 128 + 640)
        both = fast(stacked[:, lanes], high_ref[half])
        both = both[:rows] + both[rows:] + fast(high[:, lanes], low_ref[half])
        value = both[:, :128].reshape(count, 16, 128)
        value = value + factor * both[:, 128:].reshape(count, 16, 128)
        here = slice(half * 128, half * 128 + 128)
        if stage == 1:
            b_ref, out_ref = refs
            value = value * inverse
            out_ref[0:4, :, here] = value
            for i in range(4):
                taken = b_ref[4 * i : 4 * i + 1] * own_ref[4, :, here]
                for l in range(1, 4):
                    taken += b_ref[4 * i + l : 4 * i + l + 1] * own_ref[4 + l, :, here]
                out_ref[4 + i, :, here] = value[i] - inverse[0] * taken
        elif stage == 2:
            x_ref, w_ref = refs
            x_ref[:, :, here] = (value[0:4] - sigma * own_ref[0:4, :, here]) * inverse
            w_ref[:, :, here] = value[4:8] * inverse
        else:
            (out_ref,) = refs
            out_ref[:, :, here] = (value - sigma * own_ref[:, :, here]) * inverse


def share_kernel(k0, s1, k2x, k2w, k3, rest_ref, out_ref):
    total = jnp.zeros((24, 24), jnp.float32)
    for r in range(16):
        rows = jnp.concatenate(
            [k0[0:4, r, :], s1[4:8, r, :], s1[0:4, r, :], k2w[:, r, :], k2x[:, r, :], k3[:, r, :]],
            axis=0,
        )
        total += dot(rows, rows, NT)
    first = jnp.concatenate([total[0:8, 0:8] + rest_ref[:, 0:8], total[0:8, 8:24]], axis=1)
    pad = jnp.zeros((8, 8), jnp.float32)
    packed = jnp.concatenate(
        [first, pad, total[8:16], pad, total[16:24], pad, jnp.zeros((8, 32), jnp.float32)], axis=1
    )
    group = lax.broadcasted_iota(jnp.int32, (16, 128), 1) // 32
    sets = tuple([ref[c] for c in range(4)] for ref in (s1, k2w, k2x, k3))
    for m, columns in enumerate(sets):
        for half in range(2):
            tiles = [v[:, half * 128 : half * 128 + 128] for v in columns]
            for q in range(4):
                value = None
                for c in range(4):
                    by = (c - q) % 4 * 32
                    moved = pltpu.roll(tiles[c], by, 1) if by else tiles[c]
                    value = moved if value is None else jnp.where(group == c, moved, value)
                out_ref[half * 4 + q, m * 16 : m * 16 + 16] = value
    for d in range(8):
        out_ref[d, 64:72] = packed


def total_kernel(v_ref, out_ref):
    total = v_ref[0, 64:72]
    for d in range(1, 8):
        total += v_ref[d, 64:72]
    for d in range(32):
        out_ref[d] = total


def mixed(columns, rows):
    total = columns[0] * rows[0:1, :]
    for l in range(1, 4):
        total += columns[l] * rows[l : l + 1, :]
    return total


def products(a, b):
    return [jnp.sum(a * b[l : l + 1, :], axis=1, keepdims=True) for l in range(4)]


def square_of(columns):
    col = lax.broadcasted_iota(jnp.int32, (4, 4), 1)
    value = columns[0] + jnp.zeros((4, 4), jnp.float32)
    for l in range(1, 4):
        value = jnp.where(col == l, columns[l], value)
    return value


def solve_kernel(g_ref, b_ref, k_ref, v_ref, f_ref, image_ref, coef_ref, alpha_ref, beta_ref):
    lane = lax.broadcasted_iota(jnp.int32, (4, 128), 1)
    row = lax.broadcasted_iota(jnp.int32, (4, 128), 0)
    sigma, scale = k_ref[0:1, :], k_ref[2:3, :]
    packed = g_ref[0]
    for d in range(1, 32):
        packed += g_ref[d]
    narrow = lax.broadcasted_iota(jnp.int32, (8, 128), 1) < 32
    gram = jnp.concatenate(
        [
            jnp.where(narrow, packed if q == 0 else pltpu.roll(packed, 128 - 32 * q, 1), 0.0)
            for q in range(3)
        ],
        axis=0,
    )
    cur = (lane == row).astype(jnp.float32)
    cur_g = gram[0:4]
    prev = prev_g = coupling = None
    one_row = lax.broadcasted_iota(jnp.int32, (4, 1), 0)
    for step in range(3):
        if step == 0:
            w = scale * (lane == row + 4).astype(jnp.float32)
            w_g = scale * gram[4:8]
        else:
            moved = scale * pltpu.roll(jnp.where(lane < 16, cur, 0.0), 8, 1)
            moved += sigma * jnp.where(lane >= 8, cur, 0.0)
            w = moved - mixed(coupling, prev)
            w_g = dot(moved[:, 0:24], gram) - mixed(coupling, prev_g)
        across = products(w_g, cur)
        alpha_ref[step] = square_of(products(cur_g, w))
        r = w - mixed(across, cur)
        r_g = w_g - mixed(across, cur_g)
        square = products(r_g, r)
        pivots = jnp.zeros((4, 1), jnp.float32)
        for i in range(4):
            pivot = square[i][i : i + 1, :]
            pivots = jnp.where(one_row == i, pivot, pivots)
            if i < 3:
                times = jnp.where(one_row > i, square[i] / pivot, 0.0)
                r = r - times * r[i : i + 1, :]
                r_g = r_g - times * r_g[i : i + 1, :]
                square = [
                    v - times * v[i : i + 1, :] if l > i else v for l, v in enumerate(square)
                ]
        root = 1.0 / jnp.sqrt(pivots)
        upper = [jnp.where(one_row <= l, square[l] * root, 0.0) for l in range(4)]
        beta_ref[step] = square_of(upper)
        prev, prev_g, coupling = cur, cur_g, upper
        cur, cur_g = r * root, r_g * root
    coef_ref[...] = cur
    behind = cur[:, 4:5] * b_ref[0:1, :]
    for l in range(1, 4):
        behind += cur[:, 4 + l : 5 + l] * b_ref[l : l + 1, :]
    coef_ref[:, 4:8] = -k_ref[1:2, 0:1] * behind
    cur += pltpu.roll(jnp.where((lane >= 4) & (lane < 8), cur, 0.0), 4, 1)
    group = lane[0:1] // 32
    own = lane // 32 == row
    weights = [
        jnp.sum(jnp.where(own, cur[:, k : k + 1], 0.0), axis=0, keepdims=True) for k in range(8, 24)
    ]
    field = jnp.zeros((128, 128), jnp.float32)
    for m in range(4):
        tile = v_ref[:, m * 16 : m * 16 + 16].reshape(128, 128)
        for by in range(4):
            line = None
            for c in range(4):
                from_row = weights[4 * m + c]
                line = from_row if line is None else jnp.where(group == (c + by) % 4, from_row, line)
            field += line * (pltpu.roll(tile, 32 * by, 1) if by else tile)
    high, low = split(field)
    none = jnp.zeros((128, 128), jnp.bfloat16)
    right = jnp.concatenate(
        [jnp.concatenate([high, low], axis=1), jnp.concatenate([high, none], axis=1)], axis=0
    )
    both = fast(f_ref[...], right)
    image_ref[...] = (both[:, :128] + both[:, 128:]).reshape(64, 8, 128)


def last_kernel(r_ref, q_ref, coef_ref, out_ref):
    flip = odd_slab()
    group = lax.broadcasted_iota(jnp.int32, (8, 128), 1) // 32
    coef = coef_ref[...]
    scalars = [
        [coef[c : c + 1, k : k + 1] + jnp.zeros((8, 128), jnp.float32) for k in range(8)]
        for c in range(4)
    ]
    for pair in range(8):
        place = turned(pair, flip) * 8
        for half in range(2):
            lanes = slice(half * 128, half * 128 + 128)
            tiles = [r_ref[place + half * 4 + q] for q in range(4)]
            for c in range(4):
                value = None
                for q in range(4):
                    by = (q - c) % 4 * 32
                    moved = pltpu.roll(tiles[q], by, 1) if by else tiles[q]
                    value = moved if value is None else jnp.where(group == q, moved, value)
                for k in range(8):
                    value += scalars[c][k] * q_ref[place + k, :, lanes]
                out_ref[:, c, pl.ds(pair * 256 + half * 128, 128)] = value


def table(assign):
    harmonic = jnp.repeat(assign, 2)
    parity = jnp.arange(harmonic.shape[0], dtype=jnp.int32) % 2
    sectors = jnp.arange(SECTORS, dtype=jnp.int32)
    phases = (harmonic[:, None] * sectors[None, :] + 128 * parity[:, None]) % SECTORS
    weights = jnp.where(harmonic == 0, math.sqrt(1.0 / SECTORS), math.sqrt(2.0 / SECTORS))
    weights = jnp.where((harmonic == 0) & (parity == 1), 0.0, weights).astype(jnp.float32)
    return jnp.cos(2.0 * math.pi / SECTORS * phases.astype(jnp.float32)) * weights[:, None]


def ring_place(pair):
    slab, at = pair // 8 % 4, pair % 8
    return (at if slab % 2 == 0 else 7 - at) * 4 + slab


def beside(value):
    after = [(ring_place(i), ring_place(i + 1)) for i in range(32)]
    before = [(j, i) for i, j in after]
    return lax.ppermute(value, RING, after), lax.ppermute(value, RING, before)


def highest(value, step):
    return jnp.maximum(value, lax.ppermute(value, "xs", [(i, i ^ step) for i in range(4)]))


def per_device(q_block, q_prev, b_prev, stiff_blocks, couple_blocks, block_cols, assign):
    group = lax.axis_index("y") * 2 + lax.axis_index("core")

    pair = turned(lax.axis_index("z"), odd_slab()).astype(jnp.int32).reshape(1)
    packed = pack(q_block, q_prev)
    packed, pair = lax.optimization_barrier((packed, pair))
    received = lax.all_to_all(packed, SEC, 0, 0, tiled=True)

    forward, inverse = call(table_kernel, (bf16(256, 512), bf16(512, 256)), table(assign))
    factors = jnp.cos(2.0 * math.pi / SECTORS * assign.astype(jnp.float32))
    mine = lax.dynamic_slice_in_dim(factors, group * 8, 8)
    factor = jnp.broadcast_to(jnp.repeat(mine, 2)[:, None], (16, 128))
    raw = call(raw_kernel, f32(8, 128), q_block, q_prev)
    found, own_high, own_low = pl.pallas_call(
        stats_kernel,
        out_shape=(f32(8, 128), bf16(2, 640, 256), bf16(2, 640, 256)),
        grid_spec=pltpu.PrefetchScalarGridSpec(
            num_scalar_prefetch=1,
            grid=(16,),
            in_specs=[pl.BlockSpec((1, 5, 128, 128), lambda i, p: (i, 0, 0, 0))] * 2,
            out_specs=(
                pl.BlockSpec((8, 128), lambda i, p: (0, 0)),
                pl.BlockSpec((2, 640, 256), lambda i, p: (0, 0, 0)),
                pl.BlockSpec((2, 640, 256), lambda i, p: (0, 0, 0)),
            ),
            scratch_shapes=[pltpu.VMEM((6, 8, 128), jnp.float32)],
        ),
        compiler_params=pltpu.CompilerParams(vmem_limit_bytes=VMEM_LIMIT),
    )(pair, stiff_blocks, couple_blocks)
    found = highest(highest(found, 1), 2)
    sigma = 0.5 * (found[1] - found[2]) + jnp.mean(factors) * (0.5 * (found[4] - found[5]))
    scale = found[0] + found[3]
    scale = jnp.where(scale > 0, scale, 1.0)
    scales = jnp.stack([sigma, 1.0 / scale, scale] + [scale] * 5)

    b_rows = jnp.broadcast_to(b_prev.reshape(16, 1), (16, 128))
    spectrum = call(
        forward_kernel, f32(8, 16, 256), forward, received, scales, factor, b_rows
    )
    k0 = lax.all_to_all(spectrum, GROUP, 0, 0, tiled=True)

    def operator(stage, sent, value, out, *more):
        left, right = beside(sent)
        return call(
            lambda *refs: apply_kernel(stage, *refs),
            out, left, value, right, own_high, own_low, factor, scales, *more,
        )

    s1 = operator(1, k0[0:4], k0, f32(8, 16, 256), b_rows)
    rest = call(rest_kernel, f32(8, 128), k0, raw, b_prev, scales)
    k2x, k2w = operator(2, s1, s1, (f32(4, 16, 256), f32(4, 16, 256)))
    k3 = operator(3, k2w, k2w, f32(4, 16, 256))

    shares = call(share_kernel, f32(8, 72, 128), k0, s1, k2x, k2w, k3, rest)
    vectors = lax.all_to_all(shares, GROUP, 0, 0, tiled=True)
    grams = lax.all_to_all(call(total_kernel, f32(32, 8, 128), vectors), RING, 0, 0, tiled=True)
    image, coef, alphas, betas = call(
        solve_kernel,
        (f32(64, 8, 128), f32(4, 128), f32(3, 4, 4), f32(3, 4, 4)),
        grams, b_prev, scales, vectors, inverse,
    )
    back = lax.all_to_all(image, SEC, 0, 0, tiled=True)
    out = call(last_kernel, f32(8, 4, 2048), back, packed, coef)
    return out, alphas, betas


def solution(mesh):
    fine = Mesh(mesh.devices.reshape(8, 4, 2, 4), ("z", "y", "core", "xs"))
    in_specs = (
        P(SEC, None, "xs"),
        P(SEC, None, "xs"),
        P(),
        P("xs", None, None, None),
        P("xs", None, None, None),
        P("xs", None),
        P(),
    )
    out_specs = (P(SEC, None, "xs"), P(), P())
    return jax.shard_map(
        per_device, mesh=fine, in_specs=in_specs, out_specs=out_specs, check_vma=False
    )
```

```python
import math

import jax
import jax.numpy as jnp
from jax import lax
from jax.experimental import pallas as pl
from jax.experimental.pallas import tpu as pltpu
from jax.sharding import Mesh
from jax.sharding import PartitionSpec as P

HI = lax.Precision.HIGHEST
SEC = ("z", "y", "core")
GROUP = ("y", "core")
RING = ("z", "xs")
SECTORS = 512
NT = (((1,), (1,)), ((), ()))
TN = (((0,), (0,)), ((), ()))
VMEM_LIMIT = 32 * 1024 * 1024
PACK_LIMIT = 60 * 1024 * 1024


def f32(*shape):
    return jax.ShapeDtypeStruct(shape, jnp.float32)


def dot(a, b, dims=(((1,), (0,)), ((), ()))):
    return lax.dot_general(a, b, dims, precision=HI, preferred_element_type=jnp.float32)


def bf16(*shape):
    return jax.ShapeDtypeStruct(shape, jnp.bfloat16)


def split(value):
    high = value.astype(jnp.bfloat16)
    return high, (value - high.astype(jnp.float32)).astype(jnp.bfloat16)


def fast(a, b):
    return lax.dot_general(a, b, (((1,), (0,)), ((), ())), preferred_element_type=jnp.float32)


def call(kernel, out, *args):
    whole = pl.BlockSpec(memory_space=pltpu.VMEM)
    return pl.pallas_call(
        kernel,
        out_shape=out,
        in_specs=[whole] * len(args),
        out_specs=jax.tree.map(lambda _: whole, out),
        compiler_params=pltpu.CompilerParams(vmem_limit_bytes=VMEM_LIMIT),
    )(*args)


def odd_slab():
    return lax.rem(lax.axis_index("xs"), 2)


def turned(pair, flip):
    return pair + flip * (7 - 2 * pair)


def pack_kernel(q_hbm, p_hbm, out_hbm, q_ref, p_ref, o_ref, in_sem, out_sem):
    flip = odd_slab()
    arriving = []
    for i in range(4):
        lanes = pl.ds(i * 512, 512)
        both = []
        for j, (source, target) in enumerate(((q_hbm, q_ref), (p_hbm, p_ref))):
            copy = pltpu.make_async_copy(
                source.at[:, :, lanes], target.at[:, :, lanes], in_sem.at[i, j]
            )
            copy.start()
            both.append(copy)
        arriving.append(both)
    leaving = []
    for pair in range(8):
        if pair % 2 == 0:
            for copy in arriving[pair // 2]:
                copy.wait()
        lanes = pl.ds(pair * 256, 256)
        for col in range(4):
            o_ref[pair * 8 + col] = q_ref[:, col, lanes]
            o_ref[pair * 8 + 4 + col] = p_ref[:, col, lanes]
        copy = pltpu.make_async_copy(
            o_ref.at[pl.ds(pair * 8, 8)],
            out_hbm.at[pl.ds(turned(pair, flip) * 8, 8)],
            out_sem.at[pair],
        )
        copy.start()
        leaving.append(copy)
    for copy in leaving:
        copy.wait()


def pack(q_block, q_prev):
    hbm = pl.BlockSpec(memory_space=pltpu.HBM)
    return pl.pallas_call(
        pack_kernel,
        out_shape=f32(64, 8, 256),
        in_specs=[hbm, hbm],
        out_specs=hbm,
        scratch_shapes=[
            pltpu.VMEM((8, 4, 2048), jnp.float32),
            pltpu.VMEM((8, 4, 2048), jnp.float32),
            pltpu.VMEM((64, 8, 256), jnp.float32),
            pltpu.SemaphoreType.DMA((4, 2)),
            pltpu.SemaphoreType.DMA((8,)),
        ],
        compiler_params=pltpu.CompilerParams(vmem_limit_bytes=PACK_LIMIT),
    )(q_block, q_prev)


def raw_kernel(q_ref, p_ref, gram_ref):
    total = jnp.zeros((8, 8), jnp.float32)
    for s in range(8):
        rows = jnp.concatenate([q_ref[s], p_ref[s]], axis=0)
        total += dot(rows, rows, NT)
    gram_ref[...] = jnp.zeros((8, 128), jnp.float32)
    gram_ref[:, 0:8] = total


def rest_kernel(k0_ref, raw_ref, b_ref, out_ref):
    inside = jnp.zeros((8, 8), jnp.float32)
    for r in range(16):
        rows = k0_ref[:, r, :]
        inside += dot(rows, rows, NT)
    outside = raw_ref[:, 0:8] - inside
    row = lax.broadcasted_iota(jnp.int32, (4, 4), 0)
    col = lax.broadcasted_iota(jnp.int32, (4, 4), 1)
    none = jnp.zeros((4, 4), jnp.float32)
    change = jnp.concatenate(
        [
            jnp.concatenate([(row == col).astype(jnp.float32), none], axis=1),
            jnp.concatenate([none, -b_ref[...]], axis=1),
        ],
        axis=0,
    )
    out_ref[...] = jnp.zeros((8, 128), jnp.float32)
    out_ref[:, 0:8] = dot(dot(change, outside), change, NT)


def stats_kernel(pair_ref, s_ref, c_ref, out_ref, high_ref, low_ref, best_ref):
    step = pl.program_id(0)
    row = lax.broadcasted_iota(jnp.int32, (128, 128), 0)
    col = lax.broadcasted_iota(jnp.int32, (128, 128), 1)
    big = jnp.float32(3.0e38)
    found = []
    for ref in (s_ref, c_ref):
        largest = jnp.max(jnp.abs(ref[0]), axis=0)
        largest = jnp.max(largest.reshape(16, 8, 128), axis=0)
        middle = ref[0, 2]
        top = jnp.max(jnp.where(row == col, middle, -big).reshape(16, 8, 128), axis=0)
        low = jnp.max(jnp.where(row == col, -middle, -big).reshape(16, 8, 128), axis=0)
        found += [largest, top, low]

    @pl.when(step == 0)
    def _():
        for i, v in enumerate(found):
            best_ref[i] = v

    @pl.when(step > 0)
    def _():
        for i, v in enumerate(found):
            best_ref[i] = jnp.maximum(best_ref[i], v)

    @pl.when(step == 15)
    def _():
        out_ref[...] = jnp.zeros((8, 128), jnp.float32)
        for i in range(6):
            best = jnp.max(best_ref[i], axis=(0, 1), keepdims=True)
            out_ref[i : i + 1] = best + jnp.zeros((1, 128), jnp.float32)

    for half in range(2):

        @pl.when(step == pair_ref[0] * 2 + half)
        def _():
            for k in range(5):
                high, low = split(jnp.concatenate([s_ref[0, k].T, c_ref[0, k].T], axis=1))
                high_ref[half, k * 128 : k * 128 + 128] = high
                low_ref[half, k * 128 : k * 128 + 128] = low


def circle(k):
    near = ((k + 64) & 127) - 64
    quarter = ((k + 64) >> 7) & 3
    t = near.astype(jnp.float32) * (2.0 * math.pi / SECTORS)
    u = t * t
    cosine = 1.0 + u * (-1 / 2 + u * (1 / 24 + u * (-1 / 720 + u * (1 / 40320 - u * (1 / 3628800)))))
    sine = t * (1.0 + u * (-1 / 6 + u * (1 / 120 + u * (-1 / 5040 + u * (1 / 362880)))))
    value = jnp.where((quarter & 1) == 1, sine, cosine)
    return jnp.where((quarter == 1) | (quarter == 2), -value, value)


def table_kernel(h_ref, rows_ref, turned_ref, factor_ref, mean_ref, all_ref):
    harmonic = h_ref[...]
    parity = lax.broadcasted_iota(jnp.int32, (128, 128), 0) & 1
    weight = jnp.where(harmonic == 0, math.sqrt(1.0 / SECTORS), math.sqrt(2.0 / SECTORS))
    for part in range(4):
        sector = lax.broadcasted_iota(jnp.int32, (128, 128), 1) + 128 * part
        value = circle((harmonic * sector + 128 * parity) & 511) * weight
        here = slice(part * 128, part * 128 + 128)
        rows_ref[0:128, here], rows_ref[128:256, here] = split(value)
        turned_ref[here, 0:128], turned_ref[here, 128:256] = split(value.T)
    factors = circle(harmonic)
    all_ref[...] = factors
    group = lax.axis_index("y") * 2 + lax.axis_index("core")
    factor_ref[...] = all_ref[pl.ds(pl.multiple_of(group * 16, 16), 16), :]
    mean_ref[...] = jnp.sum(factors, axis=0, keepdims=True) * (1.0 / 128.0) + jnp.zeros((8, 128), jnp.float32)


def table(assign):
    vmem = pl.BlockSpec(memory_space=pltpu.VMEM)
    harmonic = jnp.broadcast_to(jnp.repeat(assign, 2)[:, None], (128, 128))
    return pl.pallas_call(
        table_kernel,
        out_shape=(bf16(256, 512), bf16(512, 256), f32(16, 128), f32(8, 128)),
        in_specs=[vmem],
        out_specs=(vmem,) * 4,
        scratch_shapes=[pltpu.VMEM((128, 128), jnp.float32)],
        cost_estimate=pl.CostEstimate(flops=0, bytes_accessed=0, transcendentals=0),
        compiler_params=pltpu.CompilerParams(vmem_limit_bytes=VMEM_LIMIT),
    )(harmonic)


def forward_kernel(f_ref, r_ref, *refs):
    out_ref = refs[-1]
    high, low = split(r_ref[...].reshape(SECTORS, 256))
    both = fast(f_ref[...], high)
    out_ref[...] = (both[:128] + both[128:] + fast(f_ref[0:128], low)).reshape(8, 16, 256)


def apply_kernel(stage, left_ref, own_ref, right_ref, high_ref, low_ref, f_ref, *refs):
    count = left_ref.shape[0]
    rows = count * 16
    wide = jnp.concatenate(
        [ref[0:count].reshape(rows, 256) for ref in (left_ref, own_ref, right_ref)], axis=1
    )
    high, low = split(wide)
    stacked = jnp.concatenate([high, low], axis=0)
    factor = f_ref[...][None]
    if stage > 1:
        k_ref, refs = refs[0], refs[1:]
        sigma, inverse = k_ref[0:1, :][None], k_ref[1:2, :][None]
    for half in range(2):
        lanes = slice(half * 128, half * 128 + 640)
        both = fast(stacked[:, lanes], high_ref[half])
        both = both[:rows] + both[rows:] + fast(high[:, lanes], low_ref[half])
        value = both[:, :128].reshape(count, 16, 128)
        value = value + factor * both[:, 128:].reshape(count, 16, 128)
        here = slice(half * 128, half * 128 + 128)
        if stage == 1:
            b_ref, out_ref = refs
            out_ref[0:4, :, here] = value
            for i in range(4):
                taken = b_ref[4 * i : 4 * i + 1] * own_ref[4, :, here]
                for l in range(1, 4):
                    taken += b_ref[4 * i + l : 4 * i + l + 1] * own_ref[4 + l, :, here]
                out_ref[4 + i, :, here] = value[i] - taken
        elif stage == 2:
            x_ref, w_ref = refs
            x_ref[:, :, here] = (value[0:4] - sigma * own_ref[0:4, :, here]) * inverse
            w_ref[:, :, here] = value[4:8] * inverse
        else:
            (out_ref,) = refs
            out_ref[:, :, here] = (value - sigma * own_ref[:, :, here]) * inverse


def share_kernel(k0, s1, k2x, k2w, k3, rest_ref, out_ref):
    total = jnp.zeros((24, 24), jnp.float32)
    for r in range(16):
        rows = jnp.concatenate(
            [k0[0:4, r, :], s1[4:8, r, :], s1[0:4, r, :], k2w[:, r, :], k2x[:, r, :], k3[:, r, :]],
            axis=0,
        )
        total += dot(rows, rows, NT)
    first = jnp.concatenate([total[0:8, 0:8] + rest_ref[:, 0:8], total[0:8, 8:24]], axis=1)
    pad = jnp.zeros((8, 8), jnp.float32)
    packed = jnp.concatenate(
        [first, pad, total[8:16], pad, total[16:24], pad, jnp.zeros((8, 32), jnp.float32)], axis=1
    )
    group = lax.broadcasted_iota(jnp.int32, (16, 128), 1) // 32
    sets = tuple([ref[c] for c in range(4)] for ref in (s1, k2w, k2x, k3))
    for m, columns in enumerate(sets):
        for half in range(2):
            tiles = [v[:, half * 128 : half * 128 + 128] for v in columns]
            for q in range(4):
                value = None
                for c in range(4):
                    by = (c - q) % 4 * 32
                    moved = pltpu.roll(tiles[c], by, 1) if by else tiles[c]
                    value = moved if value is None else jnp.where(group == c, moved, value)
                out_ref[half * 4 + q, m * 16 : m * 16 + 16] = value
    for d in range(8):
        out_ref[d, 64:72] = packed


def total_kernel(v_ref, out_ref):
    total = v_ref[0, 64:72]
    for d in range(1, 8):
        total += v_ref[d, 64:72]
    for d in range(32):
        out_ref[d] = total


def mixed(columns, rows):
    total = columns[0] * rows[0:1, :]
    for l in range(1, 4):
        total += columns[l] * rows[l : l + 1, :]
    return total


def products(a, b):
    return [jnp.sum(a * b[l : l + 1, :], axis=1, keepdims=True) for l in range(4)]


def square_of(columns):
    col = lax.broadcasted_iota(jnp.int32, (4, 4), 1)
    value = columns[0] + jnp.zeros((4, 4), jnp.float32)
    for l in range(1, 4):
        value = jnp.where(col == l, columns[l], value)
    return value


def solve_kernel(g_ref, b_ref, k_ref, v_ref, f_ref, image_ref, coef_ref, alpha_ref, beta_ref):
    lane = lax.broadcasted_iota(jnp.int32, (4, 128), 1)
    row = lax.broadcasted_iota(jnp.int32, (4, 128), 0)
    sigma, scale = k_ref[0:1, :], k_ref[2:3, :]
    packed = g_ref[0]
    for d in range(1, 32):
        packed += g_ref[d]
    narrow = lax.broadcasted_iota(jnp.int32, (8, 128), 1) < 32
    gram = jnp.concatenate(
        [
            jnp.where(narrow, packed if q == 0 else pltpu.roll(packed, 128 - 32 * q, 1), 0.0)
            for q in range(3)
        ],
        axis=0,
    )
    cur = (lane == row).astype(jnp.float32)
    cur_g = gram[0:4]
    prev = prev_g = coupling = None
    one_row = lax.broadcasted_iota(jnp.int32, (4, 1), 0)
    for step in range(3):
        if step == 0:
            w = (lane == row + 4).astype(jnp.float32)
            w_g = gram[4:8]
        else:
            moved = pltpu.roll(jnp.where(lane < 4, cur, jnp.where(lane < 16, scale * cur, 0.0)), 8, 1)
            moved += sigma * jnp.where(lane >= 8, cur, 0.0)
            w = moved - mixed(coupling, prev)
            w_g = dot(moved[:, 0:24], gram) - mixed(coupling, prev_g)
        across = products(w_g, cur)
        alpha_ref[step] = square_of(products(cur_g, w))
        r = w - mixed(across, cur)
        r_g = w_g - mixed(across, cur_g)
        square = products(r_g, r)
        pivots = jnp.zeros((4, 1), jnp.float32)
        for i in range(4):
            pivot = square[i][i : i + 1, :]
            pivots = jnp.where(one_row == i, pivot, pivots)
            if i < 3:
                times = jnp.where(one_row > i, square[i] / pivot, 0.0)
                r = r - times * r[i : i + 1, :]
                r_g = r_g - times * r_g[i : i + 1, :]
                square = [
                    v - times * v[i : i + 1, :] if l > i else v for l, v in enumerate(square)
                ]
        root = 1.0 / jnp.sqrt(pivots)
        upper = [jnp.where(one_row <= l, square[l] * root, 0.0) for l in range(4)]
        beta_ref[step] = square_of(upper)
        prev, prev_g, coupling = cur, cur_g, upper
        cur, cur_g = r * root, r_g * root
    coef_ref[...] = cur
    behind = cur[:, 4:5] * b_ref[0:1, :]
    for l in range(1, 4):
        behind += cur[:, 4 + l : 5 + l] * b_ref[l : l + 1, :]
    coef_ref[:, 4:8] = -behind
    cur += pltpu.roll(jnp.where((lane >= 4) & (lane < 8), cur, 0.0), 4, 1)
    group = lane[0:1] // 32
    own = lane // 32 == row
    weights = [
        jnp.sum(jnp.where(own, cur[:, k : k + 1], 0.0), axis=0, keepdims=True) for k in range(8, 24)
    ]
    field = jnp.zeros((128, 128), jnp.float32)
    for m in range(4):
        tile = v_ref[:, m * 16 : m * 16 + 16].reshape(128, 128)
        for by in range(4):
            line = None
            for c in range(4):
                from_row = weights[4 * m + c]
                line = from_row if line is None else jnp.where(group == (c + by) % 4, from_row, line)
            field += line * (pltpu.roll(tile, 32 * by, 1) if by else tile)
    high, low = split(field)
    none = jnp.zeros((128, 128), jnp.bfloat16)
    right = jnp.concatenate(
        [jnp.concatenate([high, low], axis=1), jnp.concatenate([high, none], axis=1)], axis=0
    )
    both = fast(f_ref[...], right)
    image_ref[...] = (both[:, :128] + both[:, 128:]).reshape(64, 8, 128)


def last_kernel(r_ref, q_ref, coef_ref, out_ref):
    flip = odd_slab()
    group = lax.broadcasted_iota(jnp.int32, (8, 128), 1) // 32
    coef = coef_ref[...]
    scalars = [
        [coef[c : c + 1, k : k + 1] + jnp.zeros((8, 128), jnp.float32) for k in range(8)]
        for c in range(4)
    ]
    for pair in range(8):
        place = turned(pair, flip) * 8
        for half in range(2):
            lanes = slice(half * 128, half * 128 + 128)
            tiles = [r_ref[place + half * 4 + q] for q in range(4)]
            for c in range(4):
                value = None
                for q in range(4):
                    by = (q - c) % 4 * 32
                    moved = pltpu.roll(tiles[q], by, 1) if by else tiles[q]
                    value = moved if value is None else jnp.where(group == q, moved, value)
                for k in range(8):
                    value += scalars[c][k] * q_ref[place + k, :, lanes]
                out_ref[:, c, pl.ds(pair * 256 + half * 128, 128)] = value


def ring_place(pair):
    slab, at = pair // 8 % 4, pair % 8
    return (at if slab % 2 == 0 else 7 - at) * 4 + slab


def beside(value):
    after = [(ring_place(i), ring_place(i + 1)) for i in range(32)]
    before = [(j, i) for i, j in after]
    return lax.ppermute(value, RING, after), lax.ppermute(value, RING, before)


def highest(value):
    others = [lax.ppermute(value, "xs", [(i, (i + k) % 4) for i in range(4)]) for k in (1, 2, 3)]
    return jnp.maximum(jnp.maximum(value, others[0]), jnp.maximum(others[1], others[2]))


def per_device(q_block, q_prev, b_prev, stiff_blocks, couple_blocks, block_cols, assign):
    pair = turned(lax.axis_index("z"), odd_slab()).astype(jnp.int32).reshape(1)
    packed = pack(q_block, q_prev)
    packed, pair = lax.optimization_barrier((packed, pair))
    received = lax.all_to_all(packed, SEC, 0, 0, tiled=True)

    forward, inverse, factor, mean = table(assign)
    raw = call(raw_kernel, f32(8, 128), q_block, q_prev)
    found, own_high, own_low = pl.pallas_call(
        stats_kernel,
        out_shape=(f32(8, 128), bf16(2, 640, 256), bf16(2, 640, 256)),
        cost_estimate=pl.CostEstimate(flops=0, bytes_accessed=0, transcendentals=0),
        grid_spec=pltpu.PrefetchScalarGridSpec(
            num_scalar_prefetch=1,
            grid=(16,),
            in_specs=[pl.BlockSpec((1, 5, 128, 128), lambda i, p: (i, 0, 0, 0))] * 2,
            out_specs=(
                pl.BlockSpec((8, 128), lambda i, p: (0, 0)),
                pl.BlockSpec((2, 640, 256), lambda i, p: (0, 0, 0)),
                pl.BlockSpec((2, 640, 256), lambda i, p: (0, 0, 0)),
            ),
            scratch_shapes=[pltpu.VMEM((6, 8, 128), jnp.float32)],
        ),
        compiler_params=pltpu.CompilerParams(vmem_limit_bytes=VMEM_LIMIT),
    )(pair, stiff_blocks, couple_blocks)
    found = highest(found)
    sigma = 0.5 * (found[1] - found[2]) + mean[0] * (0.5 * (found[4] - found[5]))
    scale = found[0] + found[3]
    scale = jnp.where(scale > 0, scale, 1.0)
    scales = jnp.stack([sigma, 1.0 / scale, scale] + [scale] * 5)

    b_rows = jnp.broadcast_to(b_prev.reshape(16, 1), (16, 128))
    spectrum = call(
        forward_kernel, f32(8, 16, 256), forward, received, scales, factor, b_rows
    )
    k0 = lax.all_to_all(spectrum, GROUP, 0, 0, tiled=True)

    def operator(stage, sent, value, out, *more):
        left, right = beside(sent)
        return call(
            lambda *refs: apply_kernel(stage, *refs),
            out, left, value, right, own_high, own_low, factor, *more,
        )

    s1 = operator(1, k0[0:4], k0, f32(8, 16, 256), b_rows)
    rest = call(rest_kernel, f32(8, 128), k0, raw, b_prev)
    k2x, k2w = operator(2, s1, s1, (f32(4, 16, 256), f32(4, 16, 256)), scales)
    k3 = operator(3, k2w, k2w, f32(4, 16, 256), scales)

    shares = call(share_kernel, f32(8, 72, 128), k0, s1, k2x, k2w, k3, rest)
    vectors = lax.all_to_all(shares, GROUP, 0, 0, tiled=True)
    grams = lax.all_to_all(call(total_kernel, f32(32, 8, 128), vectors), RING, 0, 0, tiled=True)
    image, coef, alphas, betas = call(
        solve_kernel,
        (f32(64, 8, 128), f32(4, 128), f32(3, 4, 4), f32(3, 4, 4)),
        grams, b_prev, scales, vectors, inverse,
    )
    back = lax.all_to_all(image, SEC, 0, 0, tiled=True)
    out = call(last_kernel, f32(8, 4, 2048), back, packed, coef)
    return out, alphas, betas


def solution(mesh):
    fine = Mesh(mesh.devices.reshape(8, 4, 2, 4), ("z", "y", "core", "xs"))
    in_specs = (
        P(SEC, None, "xs"),
        P(SEC, None, "xs"),
        P(),
        P("xs", None, None, None),
        P("xs", None, None, None),
        P("xs", None),
        P(),
    )
    out_specs = (P(SEC, None, "xs"), P(), P())
    return jax.shard_map(
        per_device, mesh=fine, in_specs=in_specs, out_specs=out_specs, check_vma=False
    )
```

```python
import math

import jax
import jax.numpy as jnp
from jax import lax
from jax.experimental import pallas as pl
from jax.experimental.pallas import tpu as pltpu
from jax.sharding import Mesh
from jax.sharding import PartitionSpec as P

HI = lax.Precision.HIGHEST
SEC = ("z", "y", "core")
GROUP = ("y", "core")
RING = ("z", "xs")
SECTORS = 512
NT = (((1,), (1,)), ((), ()))
TN = (((0,), (0,)), ((), ()))
VMEM_LIMIT = 32 * 1024 * 1024
PACK_LIMIT = 60 * 1024 * 1024


def f32(*shape):
    return jax.ShapeDtypeStruct(shape, jnp.float32)


def dot(a, b, dims=(((1,), (0,)), ((), ()))):
    return lax.dot_general(a, b, dims, precision=HI, preferred_element_type=jnp.float32)


def bf16(*shape):
    return jax.ShapeDtypeStruct(shape, jnp.bfloat16)


def split(value):
    high = value.astype(jnp.bfloat16)
    return high, (value - high.astype(jnp.float32)).astype(jnp.bfloat16)


def fast(a, b):
    return lax.dot_general(a, b, (((1,), (0,)), ((), ())), preferred_element_type=jnp.float32)


def call(kernel, out, *args):
    whole = pl.BlockSpec(memory_space=pltpu.VMEM)
    return pl.pallas_call(
        kernel,
        out_shape=out,
        in_specs=[whole] * len(args),
        out_specs=jax.tree.map(lambda _: whole, out),
        compiler_params=pltpu.CompilerParams(vmem_limit_bytes=VMEM_LIMIT),
    )(*args)


def odd_slab():
    return lax.rem(lax.axis_index("xs"), 2)


def turned(pair, flip):
    return pair + flip * (7 - 2 * pair)


def pack_kernel(q_hbm, p_hbm, out_hbm, q_ref, p_ref, o_ref, in_sem, out_sem):
    flip = odd_slab()
    arriving = []
    for i in range(4):
        lanes = pl.ds(i * 512, 512)
        both = []
        for j, (source, target) in enumerate(((q_hbm, q_ref), (p_hbm, p_ref))):
            copy = pltpu.make_async_copy(
                source.at[:, :, lanes], target.at[:, :, lanes], in_sem.at[i, j]
            )
            copy.start()
            both.append(copy)
        arriving.append(both)
    leaving = []
    for pair in range(8):
        if pair % 2 == 0:
            for copy in arriving[pair // 2]:
                copy.wait()
        lanes = pl.ds(pair * 256, 256)
        for col in range(4):
            o_ref[pair * 8 + col] = q_ref[:, col, lanes]
            o_ref[pair * 8 + 4 + col] = p_ref[:, col, lanes]
        copy = pltpu.make_async_copy(
            o_ref.at[pl.ds(pair * 8, 8)],
            out_hbm.at[pl.ds(turned(pair, flip) * 8, 8)],
            out_sem.at[pair],
        )
        copy.start()
        leaving.append(copy)
    for copy in leaving:
        copy.wait()


def pack(q_block, q_prev):
    hbm = pl.BlockSpec(memory_space=pltpu.HBM)
    return pl.pallas_call(
        pack_kernel,
        out_shape=f32(64, 8, 256),
        in_specs=[hbm, hbm],
        out_specs=hbm,
        scratch_shapes=[
            pltpu.VMEM((8, 4, 2048), jnp.float32),
            pltpu.VMEM((8, 4, 2048), jnp.float32),
            pltpu.VMEM((64, 8, 256), jnp.float32),
            pltpu.SemaphoreType.DMA((4, 2)),
            pltpu.SemaphoreType.DMA((8,)),
        ],
        compiler_params=pltpu.CompilerParams(vmem_limit_bytes=PACK_LIMIT),
    )(q_block, q_prev)


def raw_kernel(q_ref, p_ref, gram_ref):
    total = jnp.zeros((8, 8), jnp.float32)
    for s in range(8):
        rows = jnp.concatenate([q_ref[s], p_ref[s]], axis=0)
        total += dot(rows, rows, NT)
    gram_ref[...] = jnp.zeros((8, 128), jnp.float32)
    gram_ref[:, 0:8] = total


def rest_kernel(k0_ref, raw_ref, b_ref, out_ref):
    inside = jnp.zeros((8, 8), jnp.float32)
    for r in range(16):
        rows = k0_ref[:, r, :]
        inside += dot(rows, rows, NT)
    outside = raw_ref[:, 0:8] - inside
    row = lax.broadcasted_iota(jnp.int32, (4, 4), 0)
    col = lax.broadcasted_iota(jnp.int32, (4, 4), 1)
    none = jnp.zeros((4, 4), jnp.float32)
    change = jnp.concatenate(
        [
            jnp.concatenate([(row == col).astype(jnp.float32), none], axis=1),
            jnp.concatenate([none, -b_ref[...]], axis=1),
        ],
        axis=0,
    )
    out_ref[...] = jnp.zeros((8, 128), jnp.float32)
    out_ref[:, 0:8] = dot(dot(change, outside), change, NT)


def stats_kernel(pair_ref, s_ref, c_ref, out_ref, high_ref, low_ref, best_ref):
    step = pl.program_id(0)
    row = lax.broadcasted_iota(jnp.int32, (128, 128), 0)
    col = lax.broadcasted_iota(jnp.int32, (128, 128), 1)
    big = jnp.float32(3.0e38)
    found = []
    for ref in (s_ref, c_ref):
        largest = jnp.max(jnp.abs(ref[0]), axis=0)
        largest = jnp.max(largest.reshape(16, 8, 128), axis=0)
        middle = ref[0, 2]
        top = jnp.max(jnp.where(row == col, middle, -big).reshape(16, 8, 128), axis=0)
        low = jnp.max(jnp.where(row == col, -middle, -big).reshape(16, 8, 128), axis=0)
        found += [largest, top, low]

    @pl.when(step == 0)
    def _():
        for i, v in enumerate(found):
            best_ref[i] = v

    @pl.when(step > 0)
    def _():
        for i, v in enumerate(found):
            best_ref[i] = jnp.maximum(best_ref[i], v)

    @pl.when(step == 15)
    def _():
        out_ref[...] = jnp.zeros((8, 128), jnp.float32)
        for i in range(6):
            best = jnp.max(best_ref[i], axis=(0, 1), keepdims=True)
            out_ref[i : i + 1] = best + jnp.zeros((1, 128), jnp.float32)

    for half in range(2):

        @pl.when(step == pair_ref[0] * 2 + half)
        def _():
            for k in range(5):
                high, low = split(jnp.concatenate([s_ref[0, k].T, c_ref[0, k].T], axis=1))
                high_ref[half, k * 128 : k * 128 + 128] = high
                low_ref[half, k * 128 : k * 128 + 128] = low


def circle(k):
    near = ((k + 64) & 127) - 64
    quarter = ((k + 64) >> 7) & 3
    t = near.astype(jnp.float32) * (2.0 * math.pi / SECTORS)
    u = t * t
    cosine = 1.0 + u * (-1 / 2 + u * (1 / 24 + u * (-1 / 720 + u * (1 / 40320 - u * (1 / 3628800)))))
    sine = t * (1.0 + u * (-1 / 6 + u * (1 / 120 + u * (-1 / 5040 + u * (1 / 362880)))))
    value = jnp.where((quarter & 1) == 1, sine, cosine)
    return jnp.where((quarter == 1) | (quarter == 2), -value, value)


def table_kernel(h_ref, rows_ref, turned_ref, factor_ref, mean_ref, all_ref):
    harmonic = h_ref[...]
    parity = lax.broadcasted_iota(jnp.int32, (128, 128), 0) & 1
    weight = jnp.where(harmonic == 0, math.sqrt(1.0 / SECTORS), math.sqrt(2.0 / SECTORS))
    for part in range(4):
        sector = lax.broadcasted_iota(jnp.int32, (128, 128), 1) + 128 * part
        value = circle((harmonic * sector + 128 * parity) & 511) * weight
        here = slice(part * 128, part * 128 + 128)
        rows_ref[0:128, here], rows_ref[128:256, here] = split(value)
        turned_ref[here, 0:128], turned_ref[here, 128:256] = split(value.T)
    factors = circle(harmonic)
    all_ref[...] = factors
    group = lax.axis_index("y") * 2 + lax.axis_index("core")
    factor_ref[...] = all_ref[pl.ds(pl.multiple_of(group * 16, 16), 16), :]
    mean_ref[...] = jnp.sum(factors, axis=0, keepdims=True) * (1.0 / 128.0) + jnp.zeros((8, 128), jnp.float32)


def table(assign):
    vmem = pl.BlockSpec(memory_space=pltpu.VMEM)
    harmonic = jnp.broadcast_to(jnp.repeat(assign, 2)[:, None], (128, 128))
    return pl.pallas_call(
        table_kernel,
        out_shape=(bf16(256, 512), bf16(512, 256), f32(16, 128), f32(8, 128)),
        in_specs=[vmem],
        out_specs=(vmem,) * 4,
        scratch_shapes=[pltpu.VMEM((128, 128), jnp.float32)],
        cost_estimate=pl.CostEstimate(flops=0, bytes_accessed=0, transcendentals=0),
        compiler_params=pltpu.CompilerParams(vmem_limit_bytes=VMEM_LIMIT),
    )(harmonic)


def forward_kernel(f_ref, r_ref, *refs):
    out_ref = refs[-1]
    high, low = split(r_ref[...].reshape(SECTORS, 256))
    both = fast(f_ref[...], high)
    out_ref[...] = (both[:128] + both[128:] + fast(f_ref[0:128], low)).reshape(8, 16, 256)


def apply_kernel(stage, left_ref, own_ref, right_ref, high_ref, low_ref, f_ref, *refs):
    count = left_ref.shape[0]
    rows = count * 16
    wide = jnp.concatenate(
        [ref[0:count].reshape(rows, 256) for ref in (left_ref, own_ref, right_ref)], axis=1
    )
    high, low = split(wide)
    stacked = jnp.concatenate([high, low], axis=0)
    factor = f_ref[...][None]
    if stage > 1:
        k_ref, refs = refs[0], refs[1:]
        sigma, inverse = k_ref[0:1, :][None], k_ref[1:2, :][None]
    for half in range(2):
        lanes = slice(half * 128, half * 128 + 640)
        both = fast(stacked[:, lanes], high_ref[half])
        both = both[:rows] + both[rows:] + fast(high[:, lanes], low_ref[half])
        value = both[:, :128].reshape(count, 16, 128)
        value = value + factor * both[:, 128:].reshape(count, 16, 128)
        here = slice(half * 128, half * 128 + 128)
        if stage == 1:
            b_ref, out_ref = refs
            out_ref[0:4, :, here] = value
            for i in range(4):
                taken = b_ref[4 * i : 4 * i + 1] * own_ref[4, :, here]
                for l in range(1, 4):
                    taken += b_ref[4 * i + l : 4 * i + l + 1] * own_ref[4 + l, :, here]
                out_ref[4 + i, :, here] = value[i] - taken
        elif stage == 2:
            x_ref, w_ref = refs
            x_ref[:, :, here] = (value[0:4] - sigma * own_ref[0:4, :, here]) * inverse
            w_ref[:, :, here] = value[4:8] * inverse
        else:
            (out_ref,) = refs
            out_ref[:, :, here] = (value - sigma * own_ref[:, :, here]) * inverse


def share_kernel(k0, s1, k2x, k2w, k3, rest_ref, out_ref):
    total = jnp.zeros((24, 24), jnp.float32)
    for r in range(16):
        rows = jnp.concatenate(
            [k0[0:4, r, :], s1[4:8, r, :], s1[0:4, r, :], k2w[:, r, :], k2x[:, r, :], k3[:, r, :]],
            axis=0,
        )
        total += dot(rows, rows, NT)
    first = jnp.concatenate([total[0:8, 0:8] + rest_ref[:, 0:8], total[0:8, 8:24]], axis=1)
    pad = jnp.zeros((8, 8), jnp.float32)
    packed = jnp.concatenate(
        [first, pad, total[8:16], pad, total[16:24], pad, jnp.zeros((8, 32), jnp.float32)], axis=1
    )
    group = lax.broadcasted_iota(jnp.int32, (16, 128), 1) // 32
    sets = tuple([ref[c] for c in range(4)] for ref in (s1, k2w, k2x, k3))
    for m, columns in enumerate(sets):
        for half in range(2):
            tiles = [v[:, half * 128 : half * 128 + 128] for v in columns]
            for q in range(4):
                value = None
                for c in range(4):
                    by = (c - q) % 4 * 32
                    moved = pltpu.roll(tiles[c], by, 1) if by else tiles[c]
                    value = moved if value is None else jnp.where(group == c, moved, value)
                out_ref[half * 4 + q, m * 16 : m * 16 + 16] = value
    for d in range(8):
        out_ref[d, 64:72] = packed


def total_kernel(v_ref, out_ref):
    total = v_ref[0, 64:72]
    for d in range(1, 8):
        total += v_ref[d, 64:72]
    for d in range(32):
        out_ref[d] = total


def mixed(columns, rows):
    total = columns[0] * rows[0:1, :]
    for l in range(1, 4):
        total += columns[l] * rows[l : l + 1, :]
    return total


def products(a, b):
    return [jnp.sum(a * b[l : l + 1, :], axis=1, keepdims=True) for l in range(4)]


def square_of(columns):
    col = lax.broadcasted_iota(jnp.int32, (4, 4), 1)
    value = columns[0] + jnp.zeros((4, 4), jnp.float32)
    for l in range(1, 4):
        value = jnp.where(col == l, columns[l], value)
    return value


def solve_kernel(g_ref, b_ref, k_ref, v_ref, f_ref, image_hbm, coef_ref, alpha_ref, beta_ref, image_ref, sem):
    lane = lax.broadcasted_iota(jnp.int32, (4, 128), 1)
    row = lax.broadcasted_iota(jnp.int32, (4, 128), 0)
    sigma, scale = k_ref[0:1, :], k_ref[2:3, :]
    packed = g_ref[0]
    for d in range(1, 32):
        packed += g_ref[d]
    narrow = lax.broadcasted_iota(jnp.int32, (8, 128), 1) < 32
    gram = jnp.concatenate(
        [
            jnp.where(narrow, packed if q == 0 else pltpu.roll(packed, 128 - 32 * q, 1), 0.0)
            for q in range(3)
        ],
        axis=0,
    )
    cur = (lane == row).astype(jnp.float32)
    cur_g = gram[0:4]
    prev = prev_g = coupling = None
    one_row = lax.broadcasted_iota(jnp.int32, (4, 1), 0)
    for step in range(3):
        if step == 0:
            w = (lane == row + 4).astype(jnp.float32)
            w_g = gram[4:8]
        else:
            moved = pltpu.roll(jnp.where(lane < 4, cur, jnp.where(lane < 16, scale * cur, 0.0)), 8, 1)
            moved += sigma * jnp.where(lane >= 8, cur, 0.0)
            w = moved - mixed(coupling, prev)
            w_g = dot(moved[:, 0:24], gram) - mixed(coupling, prev_g)
        across = products(w_g, cur)
        alpha_ref[step] = square_of(products(cur_g, w))
        r = w - mixed(across, cur)
        r_g = w_g - mixed(across, cur_g)
        square = products(r_g, r)
        pivots = jnp.zeros((4, 1), jnp.float32)
        for i in range(4):
            pivot = square[i][i : i + 1, :]
            pivots = jnp.where(one_row == i, pivot, pivots)
            if i < 3:
                times = jnp.where(one_row > i, square[i] / pivot, 0.0)
                r = r - times * r[i : i + 1, :]
                r_g = r_g - times * r_g[i : i + 1, :]
                square = [
                    v - times * v[i : i + 1, :] if l > i else v for l, v in enumerate(square)
                ]
        root = 1.0 / jnp.sqrt(pivots)
        upper = [jnp.where(one_row <= l, square[l] * root, 0.0) for l in range(4)]
        beta_ref[step] = square_of(upper)
        prev, prev_g, coupling = cur, cur_g, upper
        cur, cur_g = r * root, r_g * root
    coef_ref[...] = cur
    behind = cur[:, 4:5] * b_ref[0:1, :]
    for l in range(1, 4):
        behind += cur[:, 4 + l : 5 + l] * b_ref[l : l + 1, :]
    coef_ref[:, 4:8] = -behind
    cur += pltpu.roll(jnp.where((lane >= 4) & (lane < 8), cur, 0.0), 4, 1)
    group = lane[0:1] // 32
    own = lane // 32 == row
    weights = [
        jnp.sum(jnp.where(own, cur[:, k : k + 1], 0.0), axis=0, keepdims=True) for k in range(8, 24)
    ]
    field = jnp.zeros((128, 128), jnp.float32)
    for m in range(4):
        tile = v_ref[:, m * 16 : m * 16 + 16].reshape(128, 128)
        for by in range(4):
            line = None
            for c in range(4):
                from_row = weights[4 * m + c]
                line = from_row if line is None else jnp.where(group == (c + by) % 4, from_row, line)
            field += line * (pltpu.roll(tile, 32 * by, 1) if by else tile)
    high, low = split(field)
    none = jnp.zeros((128, 128), jnp.bfloat16)
    right = jnp.concatenate(
        [jnp.concatenate([high, low], axis=1), jnp.concatenate([high, none], axis=1)], axis=0
    )
    leaving = []
    for part in range(4):
        both = fast(f_ref[part * 128 : part * 128 + 128], right)
        here = pl.ds(part * 16, 16)
        image_ref[here] = (both[:, :128] + both[:, 128:]).reshape(16, 8, 128)
        copy = pltpu.make_async_copy(image_ref.at[here], image_hbm.at[here], sem.at[part])
        copy.start()
        leaving.append(copy)
    for copy in leaving:
        copy.wait()


def last_kernel(r_ref, q_ref, coef_ref, out_hbm, out_ref, sem):
    leaving = []
    flip = odd_slab()
    group = lax.broadcasted_iota(jnp.int32, (8, 128), 1) // 32
    coef = coef_ref[...]
    scalars = [
        [coef[c : c + 1, k : k + 1] + jnp.zeros((8, 128), jnp.float32) for k in range(8)]
        for c in range(4)
    ]
    for pair in range(8):
        place = turned(pair, flip) * 8
        for half in range(2):
            lanes = slice(half * 128, half * 128 + 128)
            tiles = [r_ref[place + half * 4 + q] for q in range(4)]
            for c in range(4):
                value = None
                for q in range(4):
                    by = (q - c) % 4 * 32
                    moved = pltpu.roll(tiles[q], by, 1) if by else tiles[q]
                    value = moved if value is None else jnp.where(group == q, moved, value)
                for k in range(8):
                    value += scalars[c][k] * q_ref[place + k, :, lanes]
                out_ref[:, c, pl.ds(pair * 256 + half * 128, 128)] = value
        here = pl.ds(pair * 256, 256)
        copy = pltpu.make_async_copy(out_ref.at[:, :, here], out_hbm.at[:, :, here], sem.at[pair])
        copy.start()
        leaving.append(copy)
    for copy in leaving:
        copy.wait()


def ring_place(pair):
    slab, at = pair // 8 % 4, pair % 8
    return (at if slab % 2 == 0 else 7 - at) * 4 + slab


def beside(value):
    after = [(ring_place(i), ring_place(i + 1)) for i in range(32)]
    before = [(j, i) for i, j in after]
    return lax.ppermute(value, RING, after), lax.ppermute(value, RING, before)


def highest(value):
    others = [lax.ppermute(value, "xs", [(i, (i + k) % 4) for i in range(4)]) for k in (1, 2, 3)]
    return jnp.maximum(jnp.maximum(value, others[0]), jnp.maximum(others[1], others[2]))


def per_device(q_block, q_prev, b_prev, stiff_blocks, couple_blocks, block_cols, assign):
    pair = turned(lax.axis_index("z"), odd_slab()).astype(jnp.int32).reshape(1)
    packed = pack(q_block, q_prev)
    packed, pair = lax.optimization_barrier((packed, pair))
    received = lax.all_to_all(packed, SEC, 0, 0, tiled=True)

    forward, inverse, factor, mean = table(assign)
    raw = call(raw_kernel, f32(8, 128), q_block, q_prev)
    found, own_high, own_low = pl.pallas_call(
        stats_kernel,
        out_shape=(f32(8, 128), bf16(2, 640, 256), bf16(2, 640, 256)),
        cost_estimate=pl.CostEstimate(flops=0, bytes_accessed=0, transcendentals=0),
        grid_spec=pltpu.PrefetchScalarGridSpec(
            num_scalar_prefetch=1,
            grid=(16,),
            in_specs=[pl.BlockSpec((1, 5, 128, 128), lambda i, p: (i, 0, 0, 0))] * 2,
            out_specs=(
                pl.BlockSpec((8, 128), lambda i, p: (0, 0)),
                pl.BlockSpec((2, 640, 256), lambda i, p: (0, 0, 0)),
                pl.BlockSpec((2, 640, 256), lambda i, p: (0, 0, 0)),
            ),
            scratch_shapes=[pltpu.VMEM((6, 8, 128), jnp.float32)],
        ),
        compiler_params=pltpu.CompilerParams(vmem_limit_bytes=VMEM_LIMIT),
    )(pair, stiff_blocks, couple_blocks)
    found = highest(found)
    sigma = 0.5 * (found[1] - found[2]) + mean[0] * (0.5 * (found[4] - found[5]))
    scale = found[0] + found[3]
    scale = jnp.where(scale > 0, scale, 1.0)
    scales = jnp.stack([sigma, 1.0 / scale, scale] + [scale] * 5)

    b_rows = jnp.broadcast_to(b_prev.reshape(16, 1), (16, 128))
    spectrum = call(
        forward_kernel, f32(8, 16, 256), forward, received, scales, factor, b_rows
    )
    k0 = lax.all_to_all(spectrum, GROUP, 0, 0, tiled=True)

    def operator(stage, sent, value, out, *more):
        left, right = beside(sent)
        return call(
            lambda *refs: apply_kernel(stage, *refs),
            out, left, value, right, own_high, own_low, factor, *more,
        )

    s1 = operator(1, k0[0:4], k0, f32(8, 16, 256), b_rows)
    rest = call(rest_kernel, f32(8, 128), k0, raw, b_prev)
    k2x, k2w = operator(2, s1, s1, (f32(4, 16, 256), f32(4, 16, 256)), scales)
    k3 = operator(3, k2w, k2w, f32(4, 16, 256), scales)

    shares = call(share_kernel, f32(8, 72, 128), k0, s1, k2x, k2w, k3, rest)
    vectors = lax.all_to_all(shares, GROUP, 0, 0, tiled=True)
    grams = lax.all_to_all(call(total_kernel, f32(32, 8, 128), vectors), RING, 0, 0, tiled=True)
    vmem, hbm = (pl.BlockSpec(memory_space=space) for space in (pltpu.VMEM, pltpu.HBM))
    image, coef, alphas, betas = pl.pallas_call(
        solve_kernel,
        out_shape=(f32(64, 8, 128), f32(4, 128), f32(3, 4, 4), f32(3, 4, 4)),
        in_specs=[vmem] * 5,
        out_specs=(hbm, vmem, vmem, vmem),
        scratch_shapes=[pltpu.VMEM((64, 8, 128), jnp.float32), pltpu.SemaphoreType.DMA((4,))],
        compiler_params=pltpu.CompilerParams(vmem_limit_bytes=VMEM_LIMIT),
    )(grams, b_prev, scales, vectors, inverse)
    back = lax.all_to_all(image, SEC, 0, 0, tiled=True)
    out = pl.pallas_call(
        last_kernel,
        out_shape=f32(8, 4, 2048),
        in_specs=[vmem] * 3,
        out_specs=hbm,
        scratch_shapes=[pltpu.VMEM((8, 4, 2048), jnp.float32), pltpu.SemaphoreType.DMA((8,))],
        compiler_params=pltpu.CompilerParams(vmem_limit_bytes=VMEM_LIMIT),
    )(back, packed, coef)
    return out, alphas, betas


def solution(mesh):
    fine = Mesh(mesh.devices.reshape(8, 4, 2, 4), ("z", "y", "core", "xs"))
    in_specs = (
        P(SEC, None, "xs"),
        P(SEC, None, "xs"),
        P(),
        P("xs", None, None, None),
        P("xs", None, None, None),
        P("xs", None),
        P(),
    )
    out_specs = (P(SEC, None, "xs"), P(), P())
    return jax.shard_map(
        per_device, mesh=fine, in_specs=in_specs, out_specs=out_specs, check_vma=False
    )
```

```python
import math

import jax
import jax.numpy as jnp
from jax import lax
from jax.experimental import pallas as pl
from jax.experimental.pallas import tpu as pltpu
from jax.sharding import Mesh
from jax.sharding import PartitionSpec as P

HI = lax.Precision.HIGHEST
SEC = ("z", "y", "core")
GROUP = ("y", "core")
RING = ("z", "xs")
SECTORS = 512
NT = (((1,), (1,)), ((), ()))
TN = (((0,), (0,)), ((), ()))
VMEM_LIMIT = 32 * 1024 * 1024
PACK_LIMIT = 60 * 1024 * 1024


def f32(*shape):
    return jax.ShapeDtypeStruct(shape, jnp.float32)


def dot(a, b, dims=(((1,), (0,)), ((), ()))):
    return lax.dot_general(a, b, dims, precision=HI, preferred_element_type=jnp.float32)


def bf16(*shape):
    return jax.ShapeDtypeStruct(shape, jnp.bfloat16)


def split(value):
    high = value.astype(jnp.bfloat16)
    return high, (value - high.astype(jnp.float32)).astype(jnp.bfloat16)


def fast(a, b):
    return lax.dot_general(a, b, (((1,), (0,)), ((), ())), preferred_element_type=jnp.float32)


def call(kernel, out, *args):
    whole = pl.BlockSpec(memory_space=pltpu.VMEM)
    return pl.pallas_call(
        kernel,
        out_shape=out,
        in_specs=[whole] * len(args),
        out_specs=jax.tree.map(lambda _: whole, out),
        compiler_params=pltpu.CompilerParams(vmem_limit_bytes=VMEM_LIMIT),
    )(*args)


def odd_slab():
    return lax.rem(lax.axis_index("xs"), 2)


def turned(pair, flip):
    return pair + flip * (7 - 2 * pair)


def pack_kernel(q_hbm, p_hbm, out_hbm, q_ref, p_ref, o_ref, in_sem, out_sem):
    flip = odd_slab()
    arriving = []
    for i in range(4):
        lanes = pl.ds(i * 512, 512)
        both = []
        for j, (source, target) in enumerate(((q_hbm, q_ref), (p_hbm, p_ref))):
            copy = pltpu.make_async_copy(
                source.at[:, :, lanes], target.at[:, :, lanes], in_sem.at[i, j]
            )
            copy.start()
            both.append(copy)
        arriving.append(both)
    leaving = []
    for pair in range(8):
        if pair % 2 == 0:
            for copy in arriving[pair // 2]:
                copy.wait()
        lanes = pl.ds(pair * 256, 256)
        for col in range(4):
            o_ref[pair * 8 + col] = q_ref[:, col, lanes]
            o_ref[pair * 8 + 4 + col] = p_ref[:, col, lanes]
        copy = pltpu.make_async_copy(
            o_ref.at[pl.ds(pair * 8, 8)],
            out_hbm.at[pl.ds(turned(pair, flip) * 8, 8)],
            out_sem.at[pair],
        )
        copy.start()
        leaving.append(copy)
    for copy in leaving:
        copy.wait()


def pack(q_block, q_prev):
    hbm = pl.BlockSpec(memory_space=pltpu.HBM)
    return pl.pallas_call(
        pack_kernel,
        out_shape=f32(64, 8, 256),
        in_specs=[hbm, hbm],
        out_specs=hbm,
        scratch_shapes=[
            pltpu.VMEM((8, 4, 2048), jnp.float32),
            pltpu.VMEM((8, 4, 2048), jnp.float32),
            pltpu.VMEM((64, 8, 256), jnp.float32),
            pltpu.SemaphoreType.DMA((4, 2)),
            pltpu.SemaphoreType.DMA((8,)),
        ],
        compiler_params=pltpu.CompilerParams(vmem_limit_bytes=PACK_LIMIT),
    )(q_block, q_prev)


def raw_kernel(q_ref, p_ref, gram_ref):
    total = jnp.zeros((8, 8), jnp.float32)
    for s in range(8):
        rows = jnp.concatenate([q_ref[s], p_ref[s]], axis=0)
        total += dot(rows, rows, NT)
    gram_ref[...] = jnp.zeros((8, 128), jnp.float32)
    gram_ref[:, 0:8] = total


def rest_kernel(k0_ref, raw_ref, b_ref, out_ref):
    inside = jnp.zeros((8, 8), jnp.float32)
    for r in range(16):
        rows = k0_ref[:, r, :]
        inside += dot(rows, rows, NT)
    outside = raw_ref[:, 0:8] - inside
    row = lax.broadcasted_iota(jnp.int32, (4, 4), 0)
    col = lax.broadcasted_iota(jnp.int32, (4, 4), 1)
    none = jnp.zeros((4, 4), jnp.float32)
    change = jnp.concatenate(
        [
            jnp.concatenate([(row == col).astype(jnp.float32), none], axis=1),
            jnp.concatenate([none, -b_ref[...]], axis=1),
        ],
        axis=0,
    )
    out_ref[...] = jnp.zeros((8, 128), jnp.float32)
    out_ref[:, 0:8] = dot(dot(change, outside), change, NT)


def stats_kernel(pair_ref, s_ref, c_ref, out_ref, high_ref, low_ref, best_ref):
    step = pl.program_id(0)
    row = lax.broadcasted_iota(jnp.int32, (128, 128), 0)
    col = lax.broadcasted_iota(jnp.int32, (128, 128), 1)
    big = jnp.float32(3.0e38)
    found = []
    for ref in (s_ref, c_ref):
        largest = jnp.max(jnp.abs(ref[0]), axis=0)
        largest = jnp.max(largest.reshape(16, 8, 128), axis=0)
        middle = ref[0, 2]
        top = jnp.max(jnp.where(row == col, middle, -big).reshape(16, 8, 128), axis=0)
        low = jnp.max(jnp.where(row == col, -middle, -big).reshape(16, 8, 128), axis=0)
        found += [largest, top, low]

    @pl.when(step == 0)
    def _():
        for i, v in enumerate(found):
            best_ref[i] = v

    @pl.when(step > 0)
    def _():
        for i, v in enumerate(found):
            best_ref[i] = jnp.maximum(best_ref[i], v)

    @pl.when(step == 15)
    def _():
        out_ref[...] = jnp.zeros((8, 128), jnp.float32)
        for i in range(6):
            best = jnp.max(best_ref[i], axis=(0, 1), keepdims=True)
            out_ref[i : i + 1] = best + jnp.zeros((1, 128), jnp.float32)

    for half in range(2):

        @pl.when(step == pair_ref[0] * 2 + half)
        def _():
            for k in range(5):
                high, low = split(jnp.concatenate([s_ref[0, k].T, c_ref[0, k].T], axis=1))
                high_ref[half, k * 128 : k * 128 + 128] = high
                low_ref[half, k * 128 : k * 128 + 128] = low


def circle(k):
    near = ((k + 64) & 127) - 64
    quarter = ((k + 64) >> 7) & 3
    t = near.astype(jnp.float32) * (2.0 * math.pi / SECTORS)
    u = t * t
    cosine = 1.0 + u * (-1 / 2 + u * (1 / 24 + u * (-1 / 720 + u * (1 / 40320 - u * (1 / 3628800)))))
    sine = t * (1.0 + u * (-1 / 6 + u * (1 / 120 + u * (-1 / 5040 + u * (1 / 362880)))))
    value = jnp.where((quarter & 1) == 1, sine, cosine)
    return jnp.where((quarter == 1) | (quarter == 2), -value, value)


def table_kernel(h_ref, rows_ref, turned_ref, factor_ref, mean_ref, all_ref):
    harmonic = h_ref[...]
    parity = lax.broadcasted_iota(jnp.int32, (128, 128), 0) & 1
    weight = jnp.where(harmonic == 0, math.sqrt(1.0 / SECTORS), math.sqrt(2.0 / SECTORS))
    for part in range(4):
        sector = lax.broadcasted_iota(jnp.int32, (128, 128), 1) + 128 * part
        value = circle((harmonic * sector + 128 * parity) & 511) * weight
        here = slice(part * 128, part * 128 + 128)
        rows_ref[0:128, here], rows_ref[128:256, here] = split(value)
        turned_ref[here, 0:128], turned_ref[here, 128:256] = split(value.T)
    factors = circle(harmonic)
    all_ref[...] = factors
    group = lax.axis_index("y") * 2 + lax.axis_index("core")
    factor_ref[...] = all_ref[pl.ds(pl.multiple_of(group * 16, 16), 16), :]
    mean_ref[...] = jnp.sum(factors, axis=0, keepdims=True) * (1.0 / 128.0) + jnp.zeros((8, 128), jnp.float32)


def table(assign):
    vmem = pl.BlockSpec(memory_space=pltpu.VMEM)
    harmonic = jnp.broadcast_to(jnp.repeat(assign, 2)[:, None], (128, 128))
    return pl.pallas_call(
        table_kernel,
        out_shape=(bf16(256, 512), bf16(512, 256), f32(16, 128), f32(8, 128)),
        in_specs=[vmem],
        out_specs=(vmem,) * 4,
        scratch_shapes=[pltpu.VMEM((128, 128), jnp.float32)],
        cost_estimate=pl.CostEstimate(flops=0, bytes_accessed=0, transcendentals=0),
        compiler_params=pltpu.CompilerParams(vmem_limit_bytes=VMEM_LIMIT),
    )(harmonic)


def forward_kernel(f_ref, r_ref, *refs):
    out_ref = refs[-1]
    high, low = split(r_ref[...].reshape(SECTORS, 256))
    both = fast(f_ref[...], high)
    out_ref[...] = (both[:128] + both[128:] + fast(f_ref[0:128], low)).reshape(8, 16, 256)


def apply_kernel(stage, left_ref, own_ref, right_ref, high_ref, low_ref, f_ref, *refs):
    count = left_ref.shape[0]
    rows = count * 16
    wide = jnp.concatenate(
        [ref[0:count].reshape(rows, 256) for ref in (left_ref, own_ref, right_ref)], axis=1
    )
    high, low = split(wide)
    stacked = jnp.concatenate([high, low], axis=0)
    factor = f_ref[...][None]
    if stage > 1:
        k_ref, refs = refs[0], refs[1:]
        sigma, inverse = k_ref[0:1, :][None], k_ref[1:2, :][None]
    for half in range(2):
        lanes = slice(half * 128, half * 128 + 640)
        both = fast(stacked[:, lanes], high_ref[half])
        both = both[:rows] + both[rows:] + fast(high[:, lanes], low_ref[half])
        value = both[:, :128].reshape(count, 16, 128)
        value = value + factor * both[:, 128:].reshape(count, 16, 128)
        here = slice(half * 128, half * 128 + 128)
        if stage == 1:
            b_ref, out_ref = refs
            out_ref[0:4, :, here] = value
            for i in range(4):
                taken = b_ref[4 * i : 4 * i + 1] * own_ref[4, :, here]
                for l in range(1, 4):
                    taken += b_ref[4 * i + l : 4 * i + l + 1] * own_ref[4 + l, :, here]
                out_ref[4 + i, :, here] = value[i] - taken
        elif stage == 2:
            x_ref, w_ref = refs
            x_ref[:, :, here] = (value[0:4] - sigma * own_ref[0:4, :, here]) * inverse
            w_ref[:, :, here] = value[4:8] * inverse
        else:
            (out_ref,) = refs
            out_ref[:, :, here] = (value - sigma * own_ref[:, :, here]) * inverse


def share_kernel(k0, s1, k2x, k2w, k3, rest_ref, out_ref):
    total = jnp.zeros((24, 24), jnp.float32)
    for r in range(16):
        rows = jnp.concatenate(
            [k0[0:4, r, :], s1[4:8, r, :], s1[0:4, r, :], k2w[:, r, :], k2x[:, r, :], k3[:, r, :]],
            axis=0,
        )
        total += dot(rows, rows, NT)
    first = jnp.concatenate([total[0:8, 0:8] + rest_ref[:, 0:8], total[0:8, 8:24]], axis=1)
    pad = jnp.zeros((8, 8), jnp.float32)
    packed = jnp.concatenate(
        [first, pad, total[8:16], pad, total[16:24], pad, jnp.zeros((8, 32), jnp.float32)], axis=1
    )
    group = lax.broadcasted_iota(jnp.int32, (16, 128), 1) // 32
    sets = tuple([ref[c] for c in range(4)] for ref in (s1, k2w, k2x, k3))
    for m, columns in enumerate(sets):
        for half in range(2):
            tiles = [v[:, half * 128 : half * 128 + 128] for v in columns]
            for q in range(4):
                value = None
                for c in range(4):
                    by = (c - q) % 4 * 32
                    moved = pltpu.roll(tiles[c], by, 1) if by else tiles[c]
                    value = moved if value is None else jnp.where(group == c, moved, value)
                out_ref[half * 4 + q, m * 16 : m * 16 + 16] = value
    for d in range(8):
        out_ref[d, 64:72] = packed


def total_kernel(v_ref, out_ref):
    total = v_ref[0, 64:72]
    for d in range(1, 8):
        total += v_ref[d, 64:72]
    for d in range(32):
        out_ref[d] = total


def mixed(columns, rows):
    total = columns[0] * rows[0:1, :]
    for l in range(1, 4):
        total += columns[l] * rows[l : l + 1, :]
    return total


def products(a, b):
    return [jnp.sum(a * b[l : l + 1, :], axis=1, keepdims=True) for l in range(4)]


def square_of(columns):
    col = lax.broadcasted_iota(jnp.int32, (4, 4), 1)
    value = columns[0] + jnp.zeros((4, 4), jnp.float32)
    for l in range(1, 4):
        value = jnp.where(col == l, columns[l], value)
    return value


def solve_kernel(g_ref, b_ref, k_ref, v_ref, f_ref, image_ref, coef_ref, alpha_ref, beta_ref):
    lane = lax.broadcasted_iota(jnp.int32, (4, 128), 1)
    row = lax.broadcasted_iota(jnp.int32, (4, 128), 0)
    sigma, scale = k_ref[0:1, :], k_ref[2:3, :]
    packed = g_ref[0]
    for d in range(1, 32):
        packed += g_ref[d]
    narrow = lax.broadcasted_iota(jnp.int32, (8, 128), 1) < 32
    gram = jnp.concatenate(
        [
            jnp.where(narrow, packed if q == 0 else pltpu.roll(packed, 128 - 32 * q, 1), 0.0)
            for q in range(3)
        ],
        axis=0,
    )
    cur = (lane == row).astype(jnp.float32)
    cur_g = gram[0:4]
    prev = prev_g = coupling = None
    one_row = lax.broadcasted_iota(jnp.int32, (4, 1), 0)
    for step in range(3):
        if step == 0:
            w = (lane == row + 4).astype(jnp.float32)
            w_g = gram[4:8]
        else:
            moved = pltpu.roll(jnp.where(lane < 4, cur, jnp.where(lane < 16, scale * cur, 0.0)), 8, 1)
            moved += sigma * jnp.where(lane >= 8, cur, 0.0)
            w = moved - mixed(coupling, prev)
            w_g = dot(moved[:, 0:24], gram) - mixed(coupling, prev_g)
        across = products(w_g, cur)
        alpha_ref[step] = square_of(products(cur_g, w))
        r = w - mixed(across, cur)
        r_g = w_g - mixed(across, cur_g)
        square = products(r_g, r)
        pivots = jnp.zeros((4, 1), jnp.float32)
        for i in range(4):
            pivot = square[i][i : i + 1, :]
            pivots = jnp.where(one_row == i, pivot, pivots)
            if i < 3:
                times = jnp.where(one_row > i, square[i] / pivot, 0.0)
                r = r - times * r[i : i + 1, :]
                r_g = r_g - times * r_g[i : i + 1, :]
                square = [
                    v - times * v[i : i + 1, :] if l > i else v for l, v in enumerate(square)
                ]
        root = 1.0 / jnp.sqrt(pivots)
        upper = [jnp.where(one_row <= l, square[l] * root, 0.0) for l in range(4)]
        beta_ref[step] = square_of(upper)
        prev, prev_g, coupling = cur, cur_g, upper
        cur, cur_g = r * root, r_g * root
    coef_ref[...] = cur
    behind = cur[:, 4:5] * b_ref[0:1, :]
    for l in range(1, 4):
        behind += cur[:, 4 + l : 5 + l] * b_ref[l : l + 1, :]
    coef_ref[:, 4:8] = -behind
    cur += pltpu.roll(jnp.where((lane >= 4) & (lane < 8), cur, 0.0), 4, 1)
    group = lane[0:1] // 32
    own = lane // 32 == row
    weights = [
        jnp.sum(jnp.where(own, cur[:, k : k + 1], 0.0), axis=0, keepdims=True) for k in range(8, 24)
    ]
    field = jnp.zeros((128, 128), jnp.float32)
    for m in range(4):
        tile = v_ref[:, m * 16 : m * 16 + 16].reshape(128, 128)
        for by in range(4):
            line = None
            for c in range(4):
                from_row = weights[4 * m + c]
                line = from_row if line is None else jnp.where(group == (c + by) % 4, from_row, line)
            field += line * (pltpu.roll(tile, 32 * by, 1) if by else tile)
    high, low = split(field)
    none = jnp.zeros((128, 128), jnp.bfloat16)
    right = jnp.concatenate(
        [jnp.concatenate([high, low], axis=1), jnp.concatenate([high, none], axis=1)], axis=0
    )
    both = fast(f_ref[...], right)
    image_ref[...] = (both[:, :128] + both[:, 128:]).reshape(64, 8, 128)


def last_kernel(r_ref, q_ref, coef_ref, out_ref):
    flip = odd_slab()
    group = lax.broadcasted_iota(jnp.int32, (8, 128), 1) // 32
    coef = coef_ref[...]
    scalars = [
        [coef[c : c + 1, k : k + 1] + jnp.zeros((8, 128), jnp.float32) for k in range(8)]
        for c in range(4)
    ]
    for pair in range(8):
        place = turned(pair, flip) * 8
        for half in range(2):
            lanes = slice(half * 128, half * 128 + 128)
            tiles = [r_ref[place + half * 4 + q] for q in range(4)]
            for c in range(4):
                value = None
                for q in range(4):
                    by = (q - c) % 4 * 32
                    moved = pltpu.roll(tiles[q], by, 1) if by else tiles[q]
                    value = moved if value is None else jnp.where(group == q, moved, value)
                for k in range(8):
                    value += scalars[c][k] * q_ref[place + k, :, lanes]
                out_ref[:, c, pl.ds(pair * 256 + half * 128, 128)] = value


def ring_place(pair):
    slab, at = pair // 8 % 4, pair % 8
    return (at if slab % 2 == 0 else 7 - at) * 4 + slab


def beside(value):
    after = [(ring_place(i), ring_place(i + 1)) for i in range(32)]
    before = [(j, i) for i, j in after]
    right = lax.ppermute(value, RING, before)
    return lax.ppermute(value, RING, after), right


def highest(value):
    others = [lax.ppermute(value, "xs", [(i, (i + k) % 4) for i in range(4)]) for k in (1, 2, 3)]
    return jnp.maximum(jnp.maximum(value, others[0]), jnp.maximum(others[1], others[2]))


def per_device(q_block, q_prev, b_prev, stiff_blocks, couple_blocks, block_cols, assign):
    pair = turned(lax.axis_index("z"), odd_slab()).astype(jnp.int32).reshape(1)
    packed = pack(q_block, q_prev)
    packed, pair = lax.optimization_barrier((packed, pair))
    received = lax.all_to_all(packed, SEC, 0, 0, tiled=True)

    forward, inverse, factor, mean = table(assign)
    raw = call(raw_kernel, f32(8, 128), q_block, q_prev)
    found, own_high, own_low = pl.pallas_call(
        stats_kernel,
        out_shape=(f32(8, 128), bf16(2, 640, 256), bf16(2, 640, 256)),
        cost_estimate=pl.CostEstimate(flops=0, bytes_accessed=0, transcendentals=0),
        grid_spec=pltpu.PrefetchScalarGridSpec(
            num_scalar_prefetch=1,
            grid=(16,),
            in_specs=[pl.BlockSpec((1, 5, 128, 128), lambda i, p: (i, 0, 0, 0))] * 2,
            out_specs=(
                pl.BlockSpec((8, 128), lambda i, p: (0, 0)),
                pl.BlockSpec((2, 640, 256), lambda i, p: (0, 0, 0)),
                pl.BlockSpec((2, 640, 256), lambda i, p: (0, 0, 0)),
            ),
            scratch_shapes=[pltpu.VMEM((6, 8, 128), jnp.float32)],
        ),
        compiler_params=pltpu.CompilerParams(vmem_limit_bytes=VMEM_LIMIT),
    )(pair, stiff_blocks, couple_blocks)
    found = highest(found)
    sigma = 0.5 * (found[1] - found[2]) + mean[0] * (0.5 * (found[4] - found[5]))
    scale = found[0] + found[3]
    scale = jnp.where(scale > 0, scale, 1.0)
    scales = jnp.stack([sigma, 1.0 / scale, scale] + [scale] * 5)

    b_rows = jnp.broadcast_to(b_prev.reshape(16, 1), (16, 128))
    spectrum = call(
        forward_kernel, f32(8, 16, 256), forward, received, scales, factor, b_rows
    )
    k0 = lax.all_to_all(spectrum, GROUP, 0, 0, tiled=True)

    def operator(stage, sent, value, out, *more):
        left, right = beside(sent)
        return call(
            lambda *refs: apply_kernel(stage, *refs),
            out, left, value, right, own_high, own_low, factor, *more,
        )

    s1 = operator(1, k0[0:4], k0, f32(8, 16, 256), b_rows)
    rest = call(rest_kernel, f32(8, 128), k0, raw, b_prev)
    k2x, k2w = operator(2, s1, s1, (f32(4, 16, 256), f32(4, 16, 256)), scales)
    k3 = operator(3, k2w, k2w, f32(4, 16, 256), scales)

    shares = call(share_kernel, f32(8, 72, 128), k0, s1, k2x, k2w, k3, rest)
    vectors = lax.all_to_all(shares, GROUP, 0, 0, tiled=True)
    grams = lax.all_to_all(call(total_kernel, f32(32, 8, 128), vectors), RING, 0, 0, tiled=True)
    image, coef, alphas, betas = call(
        solve_kernel,
        (f32(64, 8, 128), f32(4, 128), f32(3, 4, 4), f32(3, 4, 4)),
        grams, b_prev, scales, vectors, inverse,
    )
    back = lax.all_to_all(image, SEC, 0, 0, tiled=True)
    out = call(last_kernel, f32(8, 4, 2048), back, packed, coef)
    return out, alphas, betas


def solution(mesh):
    fine = Mesh(mesh.devices.reshape(8, 4, 2, 4), ("z", "y", "core", "xs"))
    in_specs = (
        P(SEC, None, "xs"),
        P(SEC, None, "xs"),
        P(),
        P("xs", None, None, None),
        P("xs", None, None, None),
        P("xs", None),
        P(),
    )
    out_specs = (P(SEC, None, "xs"), P(), P())
    return jax.shard_map(
        per_device, mesh=fine, in_specs=in_specs, out_specs=out_specs, check_vma=False
    )
```
